256 devices in a mesh: prow: 16 (over y_lo, z), pcol: 16 (over x, y_hi, core).
Axes of the slice: x: 4, y: 4 (y_hi: 2, y_lo: 2; y = y_hi * 2 + y_lo), z: 8, core: 2. Of those that a mesh axis runs over, the one named last changes fastest.
Arguments:
- ancestor_inverse: bfloat16 [12288, 12288], P('pcol', 'prow'), may hold values from -0.0546875 to 0.0546875
- factor_panel: bfloat16 [3, 12288, 1024], P(None, 'prow', 'pcol'), may hold values from -1.5 to 1.5
- pattern: int32 [3, 96], replicated, may hold values 0 or 1
- diagonal_inverse: float32 [3, 1024, 1024], P(None, 'pcol', 'prow'), may hold values from -6 to 6
Outputs:
- offdiag_inverse: float32 [3, 12288, 1024], P(None, 'pcol', 'prow')
- diagonal_block: float32 [3, 1024, 1024], P(None, 'pcol', 'prow')
The draws below stay inside these ranges and needn't reach their ends.
All inputs are finite; a program needn't handle non-finite values.
Results may differ from the reference program's by a relative error of at most 0.0003.
Values may be sent and summed in bfloat16 or wider, within the bound.
No kernel may reach another device: no remote copies, remote signals or barrier semaphores. Data moves between devices by JAX's collectives and lax.ppermute only.
A program may use at most 128 MiB of HBM per device.

```python
import jax
import jax.numpy as jnp
from jax import lax

ANC = 12288
SN = 1024
BLK = 128
NSUP = 3
NBLK = 96


def touch_ends(values, rng, smallest, high):
    longest = values.shape.index(max(values.shape))
    spots = []
    for shift in (0, 1):
        where = [jax.random.randint(jax.random.fold_in(rng, axis), (), 0, length) for axis, length in enumerate(values.shape)]
        where[longest] = (where[longest] + shift) % values.shape[longest]
        spots.append(tuple(where))
    return values.at[spots[0]].set(smallest).at[spots[1]].set(high)


def steps_of(stream_key, shape, split, smallest, largest):
    gain, own = 1.0, jax.random.fold_in(stream_key, 6)
    for dim, parts in split:
        heights = jnp.exp(jax.random.uniform(jax.random.fold_in(own, dim), (parts,), jnp.float32, smallest / len(split), largest / len(split)))
        gain = gain * jnp.repeat(heights, shape[dim] // parts).reshape([-1 if axis == dim else 1 for axis in range(len(shape))])
    return gain


def bell_draw(rng, dims, scale, most, pieces=(), held_as=jnp.bfloat16):
    entries = scale * jax.random.normal(rng, dims, jnp.float32)
    if pieces:
        entries = entries * steps_of(rng, dims, pieces, -0.22, 0.18)
    return jnp.clip(entries, -most, most).astype(held_as)


def setup_inputs(seed: int = 0) -> dict:
    seeds = jax.random.split(jax.random.key(seed), 5)
    ancestor_inverse = bell_draw(seeds[0], (ANC, ANC), ANC ** -0.5, 0.0546875, ((0, 16), (1, 16)))
    factor_panel = bell_draw(seeds[1], (NSUP, ANC, SN), 0.25, 1.5, ((1, 16), (2, 16)))
    pattern = touch_ends((jax.random.randint(seeds[2], (NSUP, NBLK), 0, 3) < 2).astype(jnp.int32), jax.random.fold_in(seeds[2], 1), 0, 1)
    diagonal_inverse = bell_draw(seeds[3], (NSUP, SN, SN), 1.0, 6.0, ((1, 16), (2, 16)), jnp.float32)
    return dict(ancestor_inverse=ancestor_inverse, factor_panel=factor_panel, pattern=pattern, diagonal_inverse=diagonal_inverse)


def reference(ancestor_inverse, factor_panel, pattern, diagonal_inverse):
    spread = jnp.broadcast_to(pattern[:, :, None], (NSUP, NBLK, BLK)).reshape(NSUP, ANC).astype(jnp.float32)
    masked = (factor_panel.astype(jnp.float32) * spread[:, :, None]).astype(jnp.bfloat16)

    def product(panel):
        return jnp.dot(ancestor_inverse, panel, preferred_element_type=jnp.float32)

    reduced = lax.map(product, masked)
    offdiag = -(reduced * spread[:, :, None])
    square = jnp.einsum("kin,kim->knm", masked.astype(jnp.float32), offdiag, precision=lax.Precision.HIGHEST)
    return offdiag, diagonal_inverse - square
```

```python
import jax
import jax.numpy as jnp
import numpy as np
from jax import lax
from jax.sharding import Mesh, PartitionSpec as P

BLK = 128
AXES = ("yl", "z", "x", "yh", "core")
DIMS = (2, 8, 4, 2, 2)
GROUPS = ((0, 1, 2),)
NT = (((1,), (1,)), ((), ()))


def pairs(move):
    grid = np.arange(256).reshape(DIMS)
    return [(int(grid[at]), int(grid[move(*at)])) for at in np.ndindex(*DIMS)]


def send(value, move):
    return lax.ppermute(value, AXES, pairs(move))


def swap(yl, z, x, yh, c):
    return x // 2, z, yl * 2 + x % 2, yh, c


def swap_far(yl, z, x, yh, c):
    return x // 2, z, yl * 2 + x % 2, 1 - yh, c


def along_x(step):
    return lambda yl, z, x, yh, c: (yl, z, (x + step) % 4, yh, c)


def sibling(yl, z, x, yh, c):
    return yl, z, x, yh, 1 - c


def across(yl, z, x, yh, c):
    return 1 - yl, z, x, yh, c


def turned(yl, z, x, yh, c):
    row, col = yl * 8 + z, x * 4 + yh * 2 + c
    return col // 8, col % 8, row // 4, row // 2 % 2, row % 2


def homeward(yl, z, x, yh, c):
    slot = x * 4 + yh * 2 + c
    tile, other = slot // 2, slot % 2
    col = yl * 8 + tile
    return (yl + other) % 2, z, col // 4, col // 2 % 2, col % 2


def row_mask(pattern, block, per):
    picked = lax.dynamic_slice_in_dim(pattern, block * per, per, 1)
    return jnp.repeat(picked, BLK, axis=1)


def dot_nt(a, b):
    return lax.dot_general(a, b, NT, preferred_element_type=jnp.float32)


def ordered(first, near, far):
    return jnp.where(first, near, far), jnp.where(first, far, near)


def gather_panel(own):
    yl, x, yh, core = (lax.axis_index(name) for name in ("yl", "x", "yh", "core"))
    near, far = send(own, swap), send(own, swap_far)
    plane = jnp.stack(ordered(yh == 0, near, far))
    left, right, opposite = (send(plane, along_x(step)) for step in (1, 3, 2))
    own_rows = (x // 2) == yl
    here = ordered(own_rows, plane, opposite)
    back = (x + 3) % 4
    there = ordered((back // 2) == yl, left, right)
    halves = []
    for half in range(2):
        low, high = ordered(x % 2 == 0, here[half], there[half])
        halves.append(jnp.stack([low, high]))
    mine = jnp.stack(halves)
    theirs = send(mine, sibling)
    even, odd = ordered(core == 0, mine, theirs)
    return jnp.stack([even, odd], axis=3)


def shards(ancestor_inverse, factor_panel, pattern, diagonal_inverse):
    yl, z, x, yh, core = (lax.axis_index(name) for name in AXES)
    count, rows, cols = factor_panel.shape
    row, col = yl * 8 + z, x * 4 + yh * 2 + core
    per = rows // BLK
    keep_rows = row_mask(pattern, row, per).astype(jnp.bfloat16)
    keep_cols = row_mask(pattern, col, per).astype(jnp.float32)
    own = factor_panel.transpose(0, 2, 1) * keep_rows[:, None, :]
    beside = send(ancestor_inverse, across)
    facing = lax.all_gather(send(own, turned), "z", axis=0)
    offdiag, diagonal = [], []
    for group in GROUPS:
        size = len(group)
        span = slice(group[0], group[-1] + 1)
        panel = gather_panel(own[span]).reshape(2, 8 * size * cols, rows)
        partial = dot_nt(panel[0], ancestor_inverse) + dot_nt(panel[1], beside)
        reduced = lax.psum_scatter(partial, "z", scatter_dimension=0, tiled=True)
        reduced = reduced.reshape(size, cols, rows)
        offdiag.append(-(reduced * keep_cols[span, None, :]))
        both = jnp.stack([reduced, send(reduced, across)])
        high = lax.reduce_precision(both, 8, 7)
        tiles = 0
        for part in (high, both - high):
            tiles += jnp.einsum(
                "tknr,okmr->toknm",
                facing[:, span],
                part.astype(jnp.bfloat16),
                preferred_element_type=jnp.float32,
            )
        flat = tiles.reshape(16, size * cols * cols // 128, 128)
        summed = lax.all_to_all(flat, ("x", "yh", "core"), 0, 0, tiled=True).sum(0)
        diagonal.append(send(summed, homeward).reshape(size, cols, cols))
    offdiag = jnp.concatenate(offdiag).transpose(0, 2, 1)
    return offdiag, diagonal_inverse + jnp.concatenate(diagonal)


def solution(mesh):
    fine = Mesh(mesh.devices.reshape(DIMS), AXES)
    prow, pcol = ("yl", "z"), ("x", "yh", "core")
    in_specs = (P(pcol, prow), P(None, prow, pcol), P(), P(None, pcol, prow))
    out_specs = (P(None, pcol, prow), P(None, pcol, prow))
    return jax.shard_map(shards, mesh=fine, in_specs=in_specs, out_specs=out_specs, check_vma=False)
```

```python
import jax
import jax.numpy as jnp
import numpy as np
from jax import lax
from jax.sharding import Mesh, PartitionSpec as P

BLK = 128
AXES = ("yl", "z", "x", "yh", "core")
DIMS = (2, 8, 4, 2, 2)
NT = (((1,), (1,)), ((), ()))


def pairs(move):
    grid = np.arange(256).reshape(DIMS)
    return [(int(grid[at]), int(grid[move(*at)])) for at in np.ndindex(*DIMS)]


def send(value, move):
    return lax.ppermute(value, AXES, pairs(move))


def swap(yl, z, x, yh, c):
    return x // 2, z, yl * 2 + x % 2, yh, c


def swap_far(yl, z, x, yh, c):
    return x // 2, z, yl * 2 + x % 2, 1 - yh, c


def along_x(step):
    return lambda yl, z, x, yh, c: (yl, z, (x + step) % 4, yh, c)


def sibling(yl, z, x, yh, c):
    return yl, z, x, yh, 1 - c


def across(yl, z, x, yh, c):
    return 1 - yl, z, x, yh, c


def turned(yl, z, x, yh, c):
    row, col = yl * 8 + z, x * 4 + yh * 2 + c
    return col // 8, col % 8, row // 4, row // 2 % 2, row % 2


def turned_across(yl, z, x, yh, c):
    return across(*turned(yl, z, x, yh, c))


def row_mask(pattern, block, per):
    picked = lax.dynamic_slice_in_dim(pattern, block * per, per, 1)
    return jnp.repeat(picked, BLK, axis=1)


def dot_nt(a, b):
    return lax.dot_general(a, b, NT, preferred_element_type=jnp.float32)


def ordered(first, near, far):
    return jnp.where(first, near, far), jnp.where(first, far, near)


def after(value, *others):
    return lax.optimization_barrier((value, *others))[0]


def spread_rows(place, near, far, partly=None):
    yl, x, yh = place
    if partly is not None:
        near, far = after(near, partly), after(far, partly)
    plane = jnp.stack(ordered(yh == 0, near, far))
    left, right, opposite = (send(plane, along_x(step)) for step in (1, 3, 2))
    here = ordered((x // 2) == yl, plane, opposite)
    there = ordered(((x + 3) % 4 // 2) == yl, left, right)
    halves = [jnp.stack(ordered(x % 2 == 0, here[half], there[half])) for half in range(2)]
    return jnp.stack(halves)


def spread_cores(core, mine):
    theirs = send(mine, sibling)
    return jnp.stack(ordered(core == 0, mine, theirs), axis=3)


def shards(ancestor_inverse, factor_panel, pattern, diagonal_inverse):
    yl, z, x, yh, core = (lax.axis_index(name) for name in AXES)
    count, rows, cols = factor_panel.shape
    row, col = yl * 8 + z, x * 4 + yh * 2 + core
    per = rows // BLK
    keep_rows = row_mask(pattern, row, per).astype(jnp.bfloat16)
    keep_cols = row_mask(pattern, col, per).astype(jnp.float32)
    own = factor_panel.transpose(0, 2, 1) * keep_rows[:, None, :]
    cut = rows // 3
    top = send(ancestor_inverse[:cut], across)
    bottom = send(ancestor_inverse[cut:], across)
    offdiag, tiles = [], []
    beside = None
    for k in range(count):
        near, far = send(own[k], swap), send(own[k], swap_far)
        mine = spread_rows((yl, x, yh), near, far, top if k == 0 else None)
        if k == 0:
            mine = after(mine, bottom)
            beside = jnp.concatenate([top, bottom])
        panel = spread_cores(core, mine).reshape(2, 8 * cols, rows)
        partial = dot_nt(panel[0], ancestor_inverse) + dot_nt(panel[1], beside)
        reduced = lax.psum_scatter(partial, "z", scatter_dimension=0, tiled=True)
        offdiag.append(-(reduced * keep_cols[k, None, :]))
        high = lax.reduce_precision(reduced, 8, 7)
        parts = jnp.concatenate([high, reduced - high]).astype(jnp.bfloat16)
        square = dot_nt(panel[0], send(parts, turned)) + dot_nt(panel[1], send(parts, turned_across))
        square = square.reshape(8, 2, cols // 2, 2 * cols)
        square = square[..., :cols] + square[..., cols:]
        tiles.append(jnp.concatenate([square[:, 0], square[:, 1]], axis=-1))
    tiles = jnp.concatenate(tiles, axis=1)
    summed = lax.all_to_all(tiles, "z", 0, 0, tiled=True).sum(0)
    summed = send(summed, turned).reshape(count, cols // 2, 2 * cols)
    diagonal = jnp.concatenate([summed[..., :cols], summed[..., cols:]], axis=1)
    return jnp.stack(offdiag).transpose(0, 2, 1), diagonal_inverse + diagonal


def solution(mesh):
    fine = Mesh(mesh.devices.reshape(DIMS), AXES)
    prow, pcol = ("yl", "z"), ("x", "yh", "core")
    in_specs = (P(pcol, prow), P(None, prow, pcol), P(), P(None, pcol, prow))
    out_specs = (P(None, pcol, prow), P(None, pcol, prow))
    return jax.shard_map(shards, mesh=fine, in_specs=in_specs, out_specs=out_specs, check_vma=False)
```

```python
import jax
import jax.numpy as jnp
import numpy as np
from jax import lax
from jax.sharding import Mesh, PartitionSpec as P

BLK = 128
AXES = ("yl", "z", "x", "yh", "core")
DIMS = (2, 8, 4, 2, 2)
NT = (((1,), (1,)), ((), ()))


def pairs(move):
    grid = np.arange(256).reshape(DIMS)
    return [(int(grid[at]), int(grid[move(*at)])) for at in np.ndindex(*DIMS)]


def send(value, move):
    return lax.ppermute(value, AXES, pairs(move))


def swap(yl, z, x, yh, c):
    return x // 2, z, yl * 2 + x % 2, yh, c


def swap_far(yl, z, x, yh, c):
    return x // 2, z, yl * 2 + x % 2, 1 - yh, c


def along_x(step):
    return lambda yl, z, x, yh, c: (yl, z, (x + step) % 4, yh, c)


def along_z(step):
    return lambda yl, z, x, yh, c: (yl, (z + step) % 8, x, yh, c)


def sibling(yl, z, x, yh, c):
    return yl, z, x, yh, 1 - c


def across(yl, z, x, yh, c):
    return 1 - yl, z, x, yh, c


def turned(yl, z, x, yh, c):
    row, col = yl * 8 + z, x * 4 + yh * 2 + c
    return col // 8, col % 8, row // 4, row // 2 % 2, row % 2


def turned_across(yl, z, x, yh, c):
    return across(*turned(yl, z, x, yh, c))


def homeward(step):
    return lambda yl, z, x, yh, c: turned(yl, (z + step) % 8, x, yh, c)


def row_mask(pattern, block, per):
    picked = lax.dynamic_slice_in_dim(pattern, block * per, per, 1)
    return jnp.repeat(picked, BLK, axis=1)


def dot_nt(a, b):
    return lax.dot_general(a, b, NT, preferred_element_type=jnp.float32)


def ordered(first, near, far):
    return jnp.where(first, near, far), jnp.where(first, far, near)


def dot_each(a, b):
    return jnp.einsum("knr,kmr->knm", a, b, preferred_element_type=jnp.float32)


def spread_rows(place, near, far):
    yl, x, yh = place
    plane = jnp.stack(ordered(yh == 0, near, far), axis=1)
    left, right, opposite = (send(plane, along_x(step)) for step in (1, 3, 2))
    here = ordered((x // 2) == yl, plane, opposite)
    there = ordered(((x + 3) % 4 // 2) == yl, left, right)
    halves = [jnp.stack(ordered(x % 2 == 0, here[h], there[h]), axis=1) for h in range(2)]
    return jnp.stack(halves)


def spread_cores(core, mine):
    theirs = send(mine, sibling)
    return jnp.stack(ordered(core == 0, mine, theirs), axis=4)


def sum_over_z(z, partial):
    def block(offset):
        return lax.dynamic_index_in_dim(partial, (z + offset) % 8, 1, keepdims=False)

    half = partial.shape[2] // 2
    down = send(block(4)[:, :half], along_z(-1))
    up = send(block(4)[:, half:], along_z(1))
    below, above = block(-3), block(3)
    down = jnp.concatenate([below[:, :half] + down, below[:, half:]], axis=1)
    up = jnp.concatenate([above[:, :half], above[:, half:] + up], axis=1)
    for offset in (2, 1, 0):
        down, up = send(down, along_z(-1)), send(up, along_z(1))
        if offset:
            down, up = block(-offset) + down, block(offset) + up
    return block(0) + down + up


def shards(ancestor_inverse, factor_panel, pattern, diagonal_inverse):
    yl, z, x, yh, core = (lax.axis_index(name) for name in AXES)
    count, rows, cols = factor_panel.shape
    row, col = yl * 8 + z, x * 4 + yh * 2 + core
    per = rows // BLK
    keep_rows = row_mask(pattern, row, per).astype(jnp.bfloat16)
    keep_cols = row_mask(pattern, col, per).astype(jnp.float32)
    own = factor_panel.transpose(0, 2, 1) * keep_rows[:, None, :]
    cut, wide = rows // 3, cols // 2
    top = send(ancestor_inverse[:cut], across)
    bottom = send(ancestor_inverse[cut:], across)
    offdiag, panels, parts_own, parts_beside = [], [], [], []
    for chunk in range(2):
        piece = own[:, chunk * wide : (chunk + 1) * wide]
        near, far = send(piece, swap), send(piece, swap_far)
        if chunk == 0:
            near, far, top = lax.optimization_barrier((near, far, top))
        mine = spread_rows((yl, x, yh), near, far)
        if chunk == 0:
            mine, bottom = lax.optimization_barrier((mine, bottom))
            beside = jnp.concatenate([top, bottom])
        panel = spread_cores(core, mine).reshape(2, count, 8 * wide, rows)
        panels.append(panel)
        flat = panel.reshape(2, count * 8 * wide, rows)
        partial = dot_nt(flat[0], ancestor_inverse) + dot_nt(flat[1], beside)
        reduced = sum_over_z(z, partial.reshape(count, 8, wide, rows))
        offdiag.append(-(reduced * keep_cols[:, None, :]))
        high = lax.reduce_precision(reduced, 8, 7)
        parts = jnp.stack([high, reduced - high], axis=1).astype(jnp.bfloat16)
        parts_own.append(send(parts, turned))
        parts_beside.append(send(parts, turned_across))
    parts_own = jnp.concatenate(parts_own, axis=2).reshape(count, 2 * cols, rows)
    parts_beside = jnp.concatenate(parts_beside, axis=2).reshape(count, 2 * cols, rows)
    squares = []
    for panel in panels:
        square = dot_each(panel[0], parts_own) + dot_each(panel[1], parts_beside)
        squares.append(square[..., :cols] + square[..., cols:])
    tiles = jnp.concatenate(squares, axis=-1).reshape(count, 8, wide, 2 * cols)
    total = 0
    for step in range(8):
        tile = lax.dynamic_index_in_dim(tiles, (z + step) % 8, 1, keepdims=False)
        total += send(tile, homeward(step))
    diagonal = jnp.concatenate([total[..., :cols], total[..., cols:]], axis=1)
    return jnp.concatenate(offdiag, axis=1).transpose(0, 2, 1), diagonal_inverse + diagonal


def solution(mesh):
    fine = Mesh(mesh.devices.reshape(DIMS), AXES)
    prow, pcol = ("yl", "z"), ("x", "yh", "core")
    in_specs = (P(pcol, prow), P(None, prow, pcol), P(), P(None, pcol, prow))
    out_specs = (P(None, pcol, prow), P(None, pcol, prow))
    return jax.shard_map(shards, mesh=fine, in_specs=in_specs, out_specs=out_specs, check_vma=False)
```

```python
import jax
import jax.numpy as jnp
import numpy as np
from jax import lax
from jax.sharding import Mesh, PartitionSpec as P

BLK = 128
AXES = ("yl", "z", "x", "yh", "core")
DIMS = (2, 8, 4, 2, 2)
NT = (((1,), (1,)), ((), ()))


def pairs(move):
    grid = np.arange(256).reshape(DIMS)
    return [(int(grid[at]), int(grid[move(*at)])) for at in np.ndindex(*DIMS)]


def send(value, move):
    return lax.ppermute(value, AXES, pairs(move))


def swap(yl, z, x, yh, c):
    return x // 2, z, yl * 2 + x % 2, yh, c


def swap_far(yl, z, x, yh, c):
    return x // 2, z, yl * 2 + x % 2, 1 - yh, c


def along_x(step):
    return lambda yl, z, x, yh, c: (yl, z, (x + step) % 4, yh, c)


def along_z(step):
    return lambda yl, z, x, yh, c: (yl, (z + step) % 8, x, yh, c)


def sibling(yl, z, x, yh, c):
    return yl, z, x, yh, 1 - c


def across(yl, z, x, yh, c):
    return 1 - yl, z, x, yh, c


def skewed(yl, z, x, yh, c):
    return yl, z ^ (x % 2 * 4 + yh * 2 + c), x, yh, c


def facing_place(yl, z, x, yh, c):
    place = z ^ (x % 2 * 4 + yh * 2 + c)
    return x // 2, z, yl * 2 + place // 4, place // 2 % 2, place % 2


def beside_x(yl, z, x, yh, c):
    return yl, z, x ^ 1, yh, c


def over_y(yl, z, x, yh, c):
    return yl, z, x, 1 - yh, c


def homeward(flip):
    return lambda yl, z, x, yh, c: (yl ^ (x // 2) ^ flip, z, yl * 2 + x % 2, yh, c)


def row_mask(pattern, block, per):
    picked = lax.dynamic_slice_in_dim(pattern, block * per, per, 1)
    return jnp.repeat(picked, BLK, axis=1)


def dot_nt(a, b):
    return lax.dot_general(a, b, NT, preferred_element_type=jnp.float32)


def ordered(first, near, far):
    return jnp.where(first, near, far), jnp.where(first, far, near)


def dot_each(a, b):
    return jnp.einsum("knr,kmr->knm", a, b, preferred_element_type=jnp.float32)


def spread_rows(place, near, far):
    yl, x, yh = place
    plane = jnp.stack(ordered(yh == 0, near, far), axis=1)
    left, right, opposite = (send(plane, along_x(step)) for step in (1, 3, 2))
    here = ordered((x // 2) == yl, plane, opposite)
    there = ordered(((x + 3) % 4 // 2) == yl, left, right)
    halves = [jnp.stack(ordered(x % 2 == 0, here[h], there[h]), axis=1) for h in range(2)]
    return jnp.stack(halves)


def spread_cores(core, mine):
    theirs = send(mine, sibling)
    return jnp.stack(ordered(core == 0, mine, theirs), axis=4)


def sum_over_z(z, partial):
    def block(offset):
        return lax.dynamic_index_in_dim(partial, (z + offset) % 8, 1, keepdims=False)

    half = partial.shape[2] // 2
    down = send(block(4)[:, :half], along_z(-1))
    up = send(block(4)[:, half:], along_z(1))
    below, above = block(-3), block(3)
    down = jnp.concatenate([below[:, :half] + down, below[:, half:]], axis=1)
    up = jnp.concatenate([above[:, :half], above[:, half:] + up], axis=1)
    for offset in (2, 1, 0):
        down, up = send(down, along_z(-1)), send(up, along_z(1))
        if offset:
            down, up = block(-offset) + down, block(offset) + up
    return block(0) + down + up


def shards(ancestor_inverse, factor_panel, pattern, diagonal_inverse):
    yl, z, x, yh, core = (lax.axis_index(name) for name in AXES)
    count, rows, cols = factor_panel.shape
    row, col = yl * 8 + z, x * 4 + yh * 2 + core
    per = rows // BLK
    keep_rows = row_mask(pattern, row, per).astype(jnp.bfloat16)
    keep_cols = row_mask(pattern, col, per).astype(jnp.float32)
    own = factor_panel.transpose(0, 2, 1) * keep_rows[:, None, :]
    beside = send(ancestor_inverse, across)
    near, far = send(own, swap), send(own, swap_far)
    facing = lax.all_gather(send(send(own, skewed), facing_place), "z", axis=1)
    mine = spread_rows((yl, x, yh), near, far)
    mine, beside = lax.optimization_barrier((mine, beside))
    panel = spread_cores(core, mine).reshape(2, count * 8 * cols, rows)
    partial = dot_nt(panel[0], ancestor_inverse) + dot_nt(panel[1], beside)
    partial = partial.reshape(count, 8, cols, rows)
    wide = cols // 2
    reduced = [sum_over_z(z, partial[:, :, at : at + wide]) for at in (0, wide)]
    reduced = jnp.concatenate(reduced, axis=1)
    offdiag = -(reduced * keep_cols[:, None, :])
    high = lax.reduce_precision(reduced, 8, 7)
    parts = jnp.stack([high, reduced - high], axis=1).astype(jnp.bfloat16)
    parts = jnp.stack([parts, send(parts, across)], axis=2).reshape(count, 4 * cols, rows)
    square = dot_each(facing.reshape(count, 8 * cols, rows), parts)
    tiles = (square[..., : 2 * cols] + square[..., 2 * cols :]).reshape(count, 4, 2, cols, 2 * cols)
    tiles = tiles[:, :, 0] + send(tiles[:, :, 1], sibling)
    tiles = tiles[:, :2] + send(tiles[:, 2:], beside_x)
    tiles = tiles[:, 0] + send(tiles[:, 1], over_y)
    low, high = tiles[..., :cols], tiles[..., cols:]
    diagonal = diagonal_inverse
    for flip, picked in enumerate(ordered(x // 2 == 0, low, high)):
        packed = jnp.concatenate([picked[:, :wide], picked[:, wide:]], axis=2)
        packed = send(packed, homeward(flip))
        diagonal += jnp.concatenate([packed[..., :cols], packed[..., cols:]], axis=1)
    return offdiag.transpose(0, 2, 1), diagonal


def solution(mesh):
    fine = Mesh(mesh.devices.reshape(DIMS), AXES)
    prow, pcol = ("yl", "z"), ("x", "yh", "core")
    in_specs = (P(pcol, prow), P(None, prow, pcol), P(), P(None, pcol, prow))
    out_specs = (P(None, pcol, prow), P(None, pcol, prow))
    return jax.shard_map(shards, mesh=fine, in_specs=in_specs, out_specs=out_specs, check_vma=False)
```

```python
import jax
import jax.numpy as jnp
import numpy as np
from jax import lax
from jax.sharding import Mesh, PartitionSpec as P

BLK = 128
AXES = ("yl", "z", "x", "yh", "core")
DIMS = (2, 8, 4, 2, 2)
NT = (((1,), (1,)), ((), ()))


def pairs(move):
    grid = np.arange(256).reshape(DIMS)
    return [(int(grid[at]), int(grid[move(*at)])) for at in np.ndindex(*DIMS)]


def send(value, move):
    return lax.ppermute(value, AXES, pairs(move))


def swap(yl, z, x, yh, c):
    return x // 2, z, yl * 2 + x % 2, yh, c


def swap_far(yl, z, x, yh, c):
    return x // 2, z, yl * 2 + x % 2, 1 - yh, c


def along_x(step):
    return lambda yl, z, x, yh, c: (yl, z, (x + step) % 4, yh, c)


def along_z(step):
    return lambda yl, z, x, yh, c: (yl, (z + step) % 8, x, yh, c)


def sibling(yl, z, x, yh, c):
    return yl, z, x, yh, 1 - c


def across(yl, z, x, yh, c):
    return 1 - yl, z, x, yh, c


def skewed(yl, z, x, yh, c):
    return yl, z ^ (x % 2 * 4 + yh * 2 + c), x, yh, c


def facing_place(yl, z, x, yh, c):
    place = z ^ (x % 2 * 4 + yh * 2 + c)
    return x // 2, z, yl * 2 + place // 4, place // 2 % 2, place % 2


def over_y(yl, z, x, yh, c):
    return yl, z, x, 1 - yh, c


def flip_x(bits):
    return lambda yl, z, x, yh, c: (yl, z, x ^ bits, yh, c)


def row_mask(pattern, block, per):
    picked = lax.dynamic_slice_in_dim(pattern, block * per, per, 1)
    return jnp.repeat(picked, BLK, axis=1)


def dot_nt(a, b):
    return lax.dot_general(a, b, NT, preferred_element_type=jnp.float32)


def ordered(first, near, far):
    return jnp.where(first, near, far), jnp.where(first, far, near)


def dot_each(a, b):
    return jnp.einsum("knr,kmr->knm", a, b, preferred_element_type=jnp.float32)


def spread_rows(place, near, far):
    yl, x, yh = place
    plane = jnp.stack(ordered(yh == 0, near, far), axis=1)
    left, right = send(plane, along_x(1)), send(plane, along_x(3))
    opposite = [send(left[:, :1], along_x(1)), send(right[:, 1:], along_x(3))]
    opposite = jnp.concatenate(opposite, axis=1)
    here = ordered((x // 2) == yl, plane, opposite)
    there = ordered(((x + 3) % 4 // 2) == yl, left, right)
    halves = [jnp.stack(ordered(x % 2 == 0, here[h], there[h]), axis=1) for h in range(2)]
    return jnp.stack(halves)


def spread_cores(core, mine):
    theirs = send(mine, sibling)
    return jnp.stack(ordered(core == 0, mine, theirs), axis=4)


def sum_over_z(z, partial):
    def block(offset):
        return lax.dynamic_index_in_dim(partial, (z + offset) % 8, 1, keepdims=False)

    half = partial.shape[2] // 2
    down = send(block(4)[:, :half], along_z(-1))
    up = send(block(4)[:, half:], along_z(1))
    below, above = block(-3), block(3)
    down = jnp.concatenate([below[:, :half] + down, below[:, half:]], axis=1)
    up = jnp.concatenate([above[:, :half], above[:, half:] + up], axis=1)
    for offset in (2, 1, 0):
        down, up = send(down, along_z(-1)), send(up, along_z(1))
        if offset:
            down, up = block(-offset) + down, block(offset) + up
    return block(0) + down + up


def shards(ancestor_inverse, factor_panel, pattern, diagonal_inverse):
    yl, z, x, yh, core = (lax.axis_index(name) for name in AXES)
    count, rows, cols = factor_panel.shape
    row, col = yl * 8 + z, x * 4 + yh * 2 + core
    per = rows // BLK
    keep_rows = row_mask(pattern, row, per).astype(jnp.bfloat16)
    keep_cols = row_mask(pattern, col, per).astype(jnp.float32)
    own = factor_panel.transpose(0, 2, 1) * keep_rows[:, None, :]
    beside = send(ancestor_inverse, across)
    near, far = send(own, swap), send(own, swap_far)
    near, far, turned = lax.optimization_barrier((near, far, send(own, skewed)))
    mine = spread_rows((yl, x, yh), near, far)
    turned = send(turned, facing_place)
    mine, beside, _ = lax.optimization_barrier((mine, beside, turned))
    facing = lax.all_gather(turned, "z", axis=1)
    facing = [facing, send(facing, across)]
    panel = spread_cores(core, mine).reshape(2, count * 8 * cols, rows)
    partial = dot_nt(panel[0], ancestor_inverse) + dot_nt(panel[1], beside)
    partial = partial.reshape(count, 8, cols, rows)
    wide = cols // 2
    reduced = [sum_over_z(z, partial[:, :, at : at + wide]) for at in (0, wide)]
    reduced = jnp.concatenate(reduced, axis=1)
    offdiag = -(reduced * keep_cols[:, None, :])
    high = lax.reduce_precision(reduced, 8, 7)
    parts = jnp.stack([high, reduced - high], axis=1).astype(jnp.bfloat16)
    parts = parts.reshape(count, 2 * cols, rows)
    tiles = []
    for panel in facing:
        square = dot_each(panel.reshape(count, 8 * cols, rows), parts)
        tiles.append(square[..., :cols] + square[..., cols:])
    tiles = jnp.concatenate(tiles, axis=2).reshape(count, 2, 2, 2, cols, 2 * cols)
    tiles = tiles[:, :, :, 0] + send(tiles[:, :, :, 1], sibling)
    tiles = tiles[:, :, 0] + send(tiles[:, :, 1], over_y)
    kept, given = ordered((x // 2) == yl, tiles[..., :cols], tiles[..., cols:])
    kept, given = (jnp.concatenate([t[:, :, :wide], t[:, :, wide:]], axis=3) for t in (kept, given))
    packed = kept[:, 0] + send(kept[:, 1], flip_x(1))
    packed += send(given[:, 0], flip_x(2)) + send(given[:, 1], flip_x(3))
    diagonal = jnp.concatenate([packed[..., :cols], packed[..., cols:]], axis=1)
    diagonal += diagonal_inverse
    return offdiag.transpose(0, 2, 1), diagonal


def solution(mesh):
    fine = Mesh(mesh.devices.reshape(DIMS), AXES)
    prow, pcol = ("yl", "z"), ("x", "yh", "core")
    in_specs = (P(pcol, prow), P(None, prow, pcol), P(), P(None, pcol, prow))
    out_specs = (P(None, pcol, prow), P(None, pcol, prow))
    return jax.shard_map(shards, mesh=fine, in_specs=in_specs, out_specs=out_specs, check_vma=False)
```

```python
import jax
import jax.numpy as jnp
import numpy as np
from jax import lax
from jax.sharding import Mesh, PartitionSpec as P

BLK = 128
AXES = ("yl", "z", "x", "yh", "core")
DIMS = (2, 8, 4, 2, 2)
NT = (((1,), (1,)), ((), ()))


def pairs(move):
    grid = np.arange(256).reshape(DIMS)
    return [(int(grid[at]), int(grid[move(*at)])) for at in np.ndindex(*DIMS)]


def send(value, move):
    return lax.ppermute(value, AXES, pairs(move))


def swap(yl, z, x, yh, c):
    return x // 2, z, yl * 2 + x % 2, yh, c


def swap_far(yl, z, x, yh, c):
    return x // 2, z, yl * 2 + x % 2, 1 - yh, c


def along_x(step):
    return lambda yl, z, x, yh, c: (yl, z, (x + step) % 4, yh, c)


def along_z(step):
    return lambda yl, z, x, yh, c: (yl, (z + step) % 8, x, yh, c)


def sibling(yl, z, x, yh, c):
    return yl, z, x, yh, 1 - c


def across(yl, z, x, yh, c):
    return 1 - yl, z, x, yh, c


def skewed(yl, z, x, yh, c):
    return yl, z ^ (x % 2 * 4 + yh * 2 + c), x, yh, c


def facing_place(yl, z, x, yh, c):
    place = z ^ (x % 2 * 4 + yh * 2 + c)
    return x // 2, z, yl * 2 + place // 4, place // 2 % 2, place % 2


def over_y(yl, z, x, yh, c):
    return yl, z, x, 1 - yh, c


def flip_x(bits):
    return lambda yl, z, x, yh, c: (yl, z, x ^ bits, yh, c)


def row_mask(pattern, block, per):
    picked = lax.dynamic_slice_in_dim(pattern, block * per, per, 1)
    return jnp.repeat(picked, BLK, axis=1)


def dot_nt(a, b):
    return lax.dot_general(a, b, NT, preferred_element_type=jnp.float32)


def ordered(first, near, far):
    return jnp.where(first, near, far), jnp.where(first, far, near)


def together(*values):
    return lax.optimization_barrier(values)


def dot_each(a, b):
    return jnp.einsum("knr,kmr->knm", a, b, preferred_element_type=jnp.float32)


def spread_rows(place, plane, left, right, opposite):
    yl, x, yh = place
    opposite = jnp.concatenate(opposite, axis=1)
    here = ordered((x // 2) == yl, plane, opposite)
    there = ordered(((x + 3) % 4 // 2) == yl, left, right)
    halves = [jnp.stack(ordered(x % 2 == 0, here[h], there[h]), axis=1) for h in range(2)]
    return jnp.stack(halves)


def spread_cores(core, mine):
    theirs = send(mine, sibling)
    return jnp.stack(ordered(core == 0, mine, theirs), axis=4)


def sum_over_z(z, partial):
    def block(offset):
        return lax.dynamic_index_in_dim(partial, (z + offset) % 8, 1, keepdims=False)

    half = partial.shape[2] // 2
    down = send(block(4)[:, :half], along_z(-1))
    up = send(block(4)[:, half:], along_z(1))
    below, above = block(-3), block(3)
    down = jnp.concatenate([below[:, :half] + down, below[:, half:]], axis=1)
    up = jnp.concatenate([above[:, :half], above[:, half:] + up], axis=1)
    for offset in (2, 1, 0):
        down, up = send(down, along_z(-1)), send(up, along_z(1))
        if offset:
            down, up = block(-offset) + down, block(offset) + up
    return block(0) + down + up


def shards(ancestor_inverse, factor_panel, pattern, diagonal_inverse):
    yl, z, x, yh, core = (lax.axis_index(name) for name in AXES)
    count, rows, cols = factor_panel.shape
    row, col = yl * 8 + z, x * 4 + yh * 2 + core
    per = rows // BLK
    keep_rows = row_mask(pattern, row, per).astype(jnp.bfloat16)
    keep_cols = row_mask(pattern, col, per).astype(jnp.float32)
    own = factor_panel.transpose(0, 2, 1) * keep_rows[:, None, :]
    cuts = rows // 3, rows * 5 // 6
    beside = [send(piece, across) for piece in jnp.split(ancestor_inverse, cuts)]
    near, far = send(own, swap), send(own, swap_far)
    near, far, turned, beside[0] = together(near, far, send(own, skewed), beside[0])
    plane = jnp.stack(ordered(yh == 0, near, far), axis=1)
    left, right = send(plane, along_x(1)), send(plane, along_x(3))
    turned = send(turned, facing_place)
    left, right, turned, beside[1] = together(left, right, turned, beside[1])
    facing = lax.all_gather(turned, "z", axis=1)
    facing = [facing, send(facing, across)]
    opposite = send(left[:, :1], along_x(1)), send(right[:, 1:], along_x(3))
    *opposite, beside[2] = together(*opposite, beside[2])
    beside = jnp.concatenate(beside)
    mine = spread_rows((yl, x, yh), plane, left, right, opposite)
    panel = spread_cores(core, mine).reshape(2, count * 8 * cols, rows)
    partial = dot_nt(panel[0], ancestor_inverse) + dot_nt(panel[1], beside)
    partial = partial.reshape(count, 8, cols, rows)
    wide = cols // 2
    reduced = [sum_over_z(z, partial[:, :, at : at + wide]) for at in (0, wide)]
    reduced = jnp.concatenate(reduced, axis=1)
    offdiag = -(reduced * keep_cols[:, None, :])
    high = lax.reduce_precision(reduced, 8, 7)
    parts = jnp.stack([high, reduced - high], axis=1).astype(jnp.bfloat16)
    parts = parts.reshape(count, 2 * cols, rows)
    tiles = []
    for panel in facing:
        square = dot_each(panel.reshape(count, 8 * cols, rows), parts)
        tiles.append(square[..., :cols] + square[..., cols:])
    tiles = jnp.concatenate(tiles, axis=2).reshape(count, 2, 2, 2, cols, 2 * cols)
    tiles = tiles[:, :, :, 0] + send(tiles[:, :, :, 1], sibling)
    tiles = tiles[:, :, 0] + send(tiles[:, :, 1], over_y)
    kept, given = ordered((x // 2) == yl, tiles[..., :cols], tiles[..., cols:])
    kept, given = (jnp.concatenate([t[:, :, :wide], t[:, :, wide:]], axis=3) for t in (kept, given))
    packed = kept[:, 0] + send(kept[:, 1], flip_x(1))
    packed += send(given[:, 0], flip_x(2)) + send(given[:, 1], flip_x(3))
    diagonal = jnp.concatenate([packed[..., :cols], packed[..., cols:]], axis=1)
    diagonal += diagonal_inverse
    return offdiag.transpose(0, 2, 1), diagonal


def solution(mesh):
    fine = Mesh(mesh.devices.reshape(DIMS), AXES)
    prow, pcol = ("yl", "z"), ("x", "yh", "core")
    in_specs = (P(pcol, prow), P(None, prow, pcol), P(), P(None, pcol, prow))
    out_specs = (P(None, pcol, prow), P(None, pcol, prow))
    return jax.shard_map(shards, mesh=fine, in_specs=in_specs, out_specs=out_specs, check_vma=False)
```

```python
import jax
import jax.numpy as jnp
import numpy as np
from jax import lax
from jax.sharding import Mesh, PartitionSpec as P

BLK = 128
AXES = ("yl", "z", "x", "yh", "core")
DIMS = (2, 8, 4, 2, 2)
NT = (((1,), (1,)), ((), ()))


def pairs(move):
    grid = np.arange(256).reshape(DIMS)
    return [(int(grid[at]), int(grid[move(*at)])) for at in np.ndindex(*DIMS)]


def send(value, move):
    return lax.ppermute(value, AXES, pairs(move))


def swap(yl, z, x, yh, c):
    return (yl, z, x, yh, c) if x // 2 == yl else (1 - yl, z, 3 - x, yh, c)


def swap_far(yl, z, x, yh, c):
    return over_y(*swap(yl, z, x, yh, c))


def along_x(step):
    return lambda yl, z, x, yh, c: (yl, z, (x + step) % 4, yh, c)


def along_z(step):
    return lambda yl, z, x, yh, c: (yl, (z + step) % 8, x, yh, c)


def sibling(yl, z, x, yh, c):
    return yl, z, x, yh, 1 - c


def across(yl, z, x, yh, c):
    return 1 - yl, z, x, yh, c


def skewed(yl, z, x, yh, c):
    return yl, z ^ (x % 2 * 4 + yh * 2 + c), x, yh, c


def facing_place(yl, z, x, yh, c):
    place = z ^ (x % 2 * 4 + yh * 2 + c)
    return x // 2, z, yl * 2 + place // 4, place // 2 % 2, place % 2


def over_y(yl, z, x, yh, c):
    return yl, z, x, 1 - yh, c


def flip_x(bits):
    return lambda yl, z, x, yh, c: (yl, z, x ^ bits, yh, c)


def row_mask(pattern, block, per):
    picked = lax.dynamic_slice_in_dim(pattern, block * per, per, 1)
    return jnp.repeat(picked, BLK, axis=1)


def dot_nt(a, b):
    return lax.dot_general(a, b, NT, preferred_element_type=jnp.float32)


def ordered(first, near, far):
    return jnp.where(first, near, far), jnp.where(first, far, near)


def together(*values):
    return lax.optimization_barrier(values)


def dot_each(a, b):
    return jnp.einsum("knr,kmr->knm", a, b, preferred_element_type=jnp.float32)


def pair_rows(x, own_rows, plane, left, right, opposite):
    mirror, other = ordered(x % 2 == 0, left, right)
    here = ordered(own_rows, plane, mirror)
    there = ordered(own_rows, other, jnp.concatenate(opposite, axis=1))
    return jnp.stack([jnp.stack([here[h], there[h]], axis=1) for h in range(2)])


def sum_over_z(block, half):
    down = send(block(4)[:, :half], along_z(-1))
    up = send(block(4)[:, half:], along_z(1))
    below, above = block(-3), block(3)
    down = jnp.concatenate([below[:, :half] + down, below[:, half:]], axis=1)
    up = jnp.concatenate([above[:, :half], above[:, half:] + up], axis=1)
    for offset in (2, 1, 0):
        down, up = send(down, along_z(-1)), send(up, along_z(1))
        if offset:
            down, up = block(-offset) + down, block(offset) + up
    return block(0) + down + up


def shards(ancestor_inverse, factor_panel, pattern, diagonal_inverse):
    yl, z, x, yh, core = (lax.axis_index(name) for name in AXES)
    count, rows, cols = factor_panel.shape
    row, col = yl * 8 + z, x * 4 + yh * 2 + core
    per = rows // BLK
    keep_rows = row_mask(pattern, row, per).astype(jnp.bfloat16)
    keep_cols = row_mask(pattern, col, per).astype(jnp.float32)
    own = factor_panel.transpose(0, 2, 1) * keep_rows[:, None, :]
    cuts = rows // 3, rows * 5 // 6
    beside = [send(piece, across) for piece in jnp.split(ancestor_inverse, cuts)]
    near, far = send(own, swap), send(own, swap_far)
    near, far, turned, beside[0] = together(near, far, send(own, skewed), beside[0])
    plane = jnp.stack([near, far], axis=1)
    left, right = send(plane, along_x(1)), send(plane, along_x(3))
    turned = send(turned, facing_place)
    left, right, turned, beside[1] = together(left, right, turned, beside[1])
    facing = lax.all_gather(turned, "z", axis=1)
    facing = [facing, None]
    opposite = send(left[:, :1], along_x(1)), send(right[:, 1:], along_x(3))
    *opposite, beside[2] = together(*opposite, beside[2])
    beside = jnp.concatenate(beside)
    own_rows = (x // 2) == yl
    mine = pair_rows(x, own_rows, plane, left, right, opposite)

    def product(panel):
        panel = panel.reshape(2, count * 4 * cols, rows)
        whole = dot_nt(panel[0], ancestor_inverse) + dot_nt(panel[1], beside)
        return whole.reshape(count, 4, cols, rows)

    theirs = send(mine, sibling)
    near, far, facing[0] = together(product(mine), product(theirs), facing[0])
    facing[1] = send(facing[0], across)
    column = jnp.where(own_rows, x % 2, 1 - x % 2)
    wide = cols // 2

    def block(first, offset):
        place = (z + offset) % 8
        at = (place // 4 ^ column) * 2 + (place // 2 % 2 ^ yh)
        start, size = (0, at, first, 0), (count, 1, wide, rows)
        picked = (lax.dynamic_slice(side, start, size) for side in (near, far))
        return jnp.where(place % 2 == core, *picked).reshape(count, wide, rows)

    reduced = [
        sum_over_z(lambda offset, first=first: block(first, offset), wide // 2) for first in (0, wide)
    ]
    reduced = jnp.concatenate(reduced, axis=1)
    offdiag = -(reduced * keep_cols[:, None, :])
    high = lax.reduce_precision(reduced, 8, 7)
    parts = jnp.stack([high, reduced - high], axis=1).astype(jnp.bfloat16)
    parts = parts.reshape(count, 2 * cols, rows)
    tiles = []
    for panel in facing:
        square = dot_each(panel.reshape(count, 8 * cols, rows), parts)
        tiles.append(square[..., :cols] + square[..., cols:])
    tiles = jnp.concatenate(tiles, axis=2).reshape(count, 2, 2, 2, cols, 2 * cols)
    tiles = tiles[:, :, :, 0] + send(tiles[:, :, :, 1], sibling)
    kept, given = ordered((x // 2) == yl, tiles[..., :cols], tiles[..., cols:])
    kept, given = (jnp.concatenate([t[:, :, :, :wide], t[:, :, :, wide:]], axis=4) for t in (kept, given))
    packed = kept[:, 0] + send(kept[:, 1], flip_x(1))
    packed += send(given[:, 0], flip_x(2)) + send(given[:, 1], flip_x(3))
    packed = packed[:, 0] + send(packed[:, 1], over_y)
    diagonal = jnp.concatenate([packed[..., :cols], packed[..., cols:]], axis=1)
    diagonal += diagonal_inverse
    return offdiag.transpose(0, 2, 1), diagonal


def solution(mesh):
    fine = Mesh(mesh.devices.reshape(DIMS), AXES)
    prow, pcol = ("yl", "z"), ("x", "yh", "core")
    in_specs = (P(pcol, prow), P(None, prow, pcol), P(), P(None, pcol, prow))
    out_specs = (P(None, pcol, prow), P(None, pcol, prow))
    return jax.shard_map(shards, mesh=fine, in_specs=in_specs, out_specs=out_specs, check_vma=False)
```

```python
import jax
import jax.numpy as jnp
import numpy as np
from jax import lax
from jax.sharding import Mesh, PartitionSpec as P

BLK = 128
AXES = ("yl", "z", "x", "yh", "core")
DIMS = (2, 8, 4, 2, 2)
NT = (((1,), (1,)), ((), ()))


def pairs(move):
    grid = np.arange(256).reshape(DIMS)
    return [(int(grid[at]), int(grid[move(*at)])) for at in np.ndindex(*DIMS)]


def send(value, move):
    return lax.ppermute(value, AXES, pairs(move))


def swap(yl, z, x, yh, c):
    return (yl, z, x, yh, c) if x // 2 == yl else (1 - yl, z, 3 - x, yh, c)


def swap_far(yl, z, x, yh, c):
    return over_y(*swap(yl, z, x, yh, c))


def along_x(step):
    return lambda yl, z, x, yh, c: (yl, z, (x + step) % 4, yh, c)


def along_z(step):
    return lambda yl, z, x, yh, c: (yl, (z + step) % 8, x, yh, c)


def sibling(yl, z, x, yh, c):
    return yl, z, x, yh, 1 - c


def across(yl, z, x, yh, c):
    return 1 - yl, z, x, yh, c


def skewed(yl, z, x, yh, c):
    return yl, z ^ (x % 2 * 4 + yh * 2 + c), x, yh, c


def facing_place(yl, z, x, yh, c):
    place = z ^ (x % 2 * 4 + yh * 2 + c)
    return x // 2, z, yl * 2 + place // 4, place // 2 % 2, place % 2


def over_y(yl, z, x, yh, c):
    return yl, z, x, 1 - yh, c


def flip_x(bits):
    return lambda yl, z, x, yh, c: (yl, z, x ^ bits, yh, c)


def row_mask(pattern, block, per):
    picked = lax.dynamic_slice_in_dim(pattern, block * per, per, 1)
    return jnp.repeat(picked, BLK, axis=1)


def dot_nt(a, b):
    return lax.dot_general(a, b, NT, preferred_element_type=jnp.float32)


def ordered(first, near, far):
    return jnp.where(first, near, far), jnp.where(first, far, near)


def together(*values):
    return lax.optimization_barrier(values)


def dot_each(a, b):
    return jnp.einsum("knr,kmr->knm", a, b, preferred_element_type=jnp.float32)


def pair_rows(x, own_rows, plane, left, right, opposite):
    mirror, other = ordered(x % 2 == 0, left, right)
    here = ordered(own_rows, plane, mirror)
    there = ordered(own_rows, other, jnp.concatenate(opposite, axis=1))
    return jnp.stack([jnp.stack([here[h], there[h]], axis=1) for h in range(2)])


def sum_over_z(block, half):
    down = send(block(4)[:, :half], along_z(-1))
    up = send(block(4)[:, half:], along_z(1))
    below, above = block(-3), block(3)
    down = jnp.concatenate([below[:, :half] + down, below[:, half:]], axis=1)
    up = jnp.concatenate([above[:, :half], above[:, half:] + up], axis=1)
    for offset in (2, 1, 0):
        down, up = send(down, along_z(-1)), send(up, along_z(1))
        if offset:
            down, up = block(-offset) + down, block(offset) + up
    return block(0) + down + up


def shards(ancestor_inverse, factor_panel, pattern, diagonal_inverse):
    yl, z, x, yh, core = (lax.axis_index(name) for name in AXES)
    count, rows, cols = factor_panel.shape
    row, col = yl * 8 + z, x * 4 + yh * 2 + core
    per = rows // BLK
    keep_rows = row_mask(pattern, row, per).astype(jnp.bfloat16)
    keep_cols = row_mask(pattern, col, per).astype(jnp.float32)
    own = factor_panel.transpose(0, 2, 1) * keep_rows[:, None, :]
    near, far = send(own, swap), send(own, swap_far)
    near, far, turned, ancestor = together(near, far, send(own, skewed), ancestor_inverse)
    beside = [send(piece, across) for piece in jnp.split(ancestor, (rows // 2, rows * 5 // 6))]
    plane = jnp.stack([near, far], axis=1)
    left, right = send(plane, along_x(1)), send(plane, along_x(3))
    turned = send(turned, facing_place)
    left, right, _, beside[0] = together(left, right, turned, beside[0])
    facing = [lax.all_gather(turned, "z", axis=1), None]
    opposite = send(left[:, :1], along_x(1)), send(right[:, 1:], along_x(3))
    *opposite, beside[1] = together(*opposite, beside[1])
    own_rows = (x // 2) == yl
    mine = pair_rows(x, own_rows, plane, left, right, opposite)

    def product(panel):
        panel = panel.reshape(2, count * 4 * cols, rows)
        whole = dot_nt(panel[0], ancestor_inverse) + dot_nt(panel[1], beside)
        return whole.reshape(count, 4, cols, rows)

    theirs, beside[2] = together(send(mine, sibling), beside[2])
    beside = jnp.concatenate(beside)
    near, far, facing[0] = together(product(mine), product(theirs), facing[0])
    facing[1] = send(facing[0], across)
    column = jnp.where(own_rows, x % 2, 1 - x % 2)
    wide = cols // 2

    def block(first, offset):
        place = (z + offset) % 8
        at = (place // 4 ^ column) * 2 + (place // 2 % 2 ^ yh)
        start, size = (0, at, first, 0), (count, 1, wide, rows)
        picked = (lax.dynamic_slice(side, start, size) for side in (near, far))
        return jnp.where(place % 2 == core, *picked).reshape(count, wide, rows)

    reduced = [
        sum_over_z(lambda offset, first=first: block(first, offset), wide // 2) for first in (0, wide)
    ]
    reduced = jnp.concatenate(reduced, axis=1)
    offdiag = -(reduced * keep_cols[:, None, :])
    high = lax.reduce_precision(reduced, 8, 7)
    parts = jnp.stack([high, reduced - high], axis=1).astype(jnp.bfloat16)
    parts = parts.reshape(count, 2 * cols, rows)
    tiles = []
    for panel in facing:
        square = dot_each(panel.reshape(count, 8 * cols, rows), parts)
        tiles.append(square[..., :cols] + square[..., cols:])
    tiles = jnp.concatenate(tiles, axis=2).reshape(count, 2, 2, 2, cols, 2 * cols)
    tiles = tiles[:, :, :, 0] + send(tiles[:, :, :, 1], sibling)
    kept, given = ordered((x // 2) == yl, tiles[..., :cols], tiles[..., cols:])
    kept, given = (jnp.concatenate([t[:, :, :, :wide], t[:, :, :, wide:]], axis=4) for t in (kept, given))
    packed = kept[:, 0] + send(kept[:, 1], flip_x(1))
    packed += send(given[:, 0], flip_x(2)) + send(given[:, 1], flip_x(3))
    packed = packed[:, 0] + send(packed[:, 1], over_y)
    diagonal = jnp.concatenate([packed[..., :cols], packed[..., cols:]], axis=1)
    diagonal += diagonal_inverse
    return offdiag.transpose(0, 2, 1), diagonal


def solution(mesh):
    fine = Mesh(mesh.devices.reshape(DIMS), AXES)
    prow, pcol = ("yl", "z"), ("x", "yh", "core")
    in_specs = (P(pcol, prow), P(None, prow, pcol), P(), P(None, pcol, prow))
    out_specs = (P(None, pcol, prow), P(None, pcol, prow))
    return jax.shard_map(shards, mesh=fine, in_specs=in_specs, out_specs=out_specs, check_vma=False)
```

```python
import jax
import jax.numpy as jnp
import numpy as np
from jax import lax
from jax.sharding import Mesh, PartitionSpec as P

BLK = 128
AXES = ("yl", "z", "x", "yh", "core")
DIMS = (2, 8, 4, 2, 2)
NT = (((1,), (1,)), ((), ()))


def pairs(move):
    grid = np.arange(256).reshape(DIMS)
    return [(int(grid[at]), int(grid[move(*at)])) for at in np.ndindex(*DIMS)]


def send(value, move):
    return lax.ppermute(value, AXES, pairs(move))


def swap(yl, z, x, yh, c):
    return (yl, z, x, yh, c) if x // 2 == yl else (1 - yl, z, 3 - x, yh, c)


def swap_far(yl, z, x, yh, c):
    return over_y(*swap(yl, z, x, yh, c))


def along_x(step):
    return lambda yl, z, x, yh, c: (yl, z, (x + step) % 4, yh, c)


def along_z(step):
    return lambda yl, z, x, yh, c: (yl, (z + step) % 8, x, yh, c)


def sibling(yl, z, x, yh, c):
    return yl, z, x, yh, 1 - c


def across(yl, z, x, yh, c):
    return 1 - yl, z, x, yh, c


def skewed(yl, z, x, yh, c):
    return yl, z ^ (x % 2 * 4 + yh * 2 + c), x, yh, c


def facing_place(yl, z, x, yh, c):
    place = z ^ (x % 2 * 4 + yh * 2 + c)
    return x // 2, z, yl * 2 + place // 4, place // 2 % 2, place % 2


def over_y(yl, z, x, yh, c):
    return yl, z, x, 1 - yh, c


def flip_x(bits):
    return lambda yl, z, x, yh, c: (yl, z, x ^ bits, yh, c)


def row_mask(pattern, block, per):
    picked = lax.dynamic_slice_in_dim(pattern, block * per, per, 1)
    return jnp.repeat(picked, BLK, axis=1)


def dot_nt(a, b):
    return lax.dot_general(a, b, NT, preferred_element_type=jnp.float32)


def ordered(first, near, far):
    return jnp.where(first, near, far), jnp.where(first, far, near)


def together(*values):
    return lax.optimization_barrier(values)


def dot_each(a, b):
    return jnp.einsum("knr,kmr->knm", a, b, preferred_element_type=jnp.float32)


def pair_rows(x, own_rows, plane, left, right, opposite):
    mirror, other = ordered(x % 2 == 0, left, right)
    here = ordered(own_rows, plane, mirror)
    there = ordered(own_rows, other, jnp.concatenate(opposite, axis=1))
    return jnp.stack([jnp.stack([here[h], there[h]], axis=1) for h in range(2)])


def with_own(block, half, offset, down, up):
    below, above = block(-offset), block(offset)
    if offset < 3:
        return below + down, above + up
    down = jnp.concatenate([below[:, :half] + down, below[:, half:]], axis=1)
    up = jnp.concatenate([above[:, :half], above[:, half:] + up], axis=1)
    return down, up


def sum_over_z(first, second, half, extra):
    def both_ways(pair):
        return send(pair[0], along_z(-1)), send(pair[1], along_z(1))

    def behind(pair, *others):
        return together(*pair, *others)[:2]

    one, two = ((block(4)[:, :half], block(4)[:, half:]) for block in (first, second))
    for offset in (3, 2, 1):
        got = both_ways(one)
        if offset == 3:
            *got, extra = together(*got, extra)
        one = with_own(first, half, offset, *behind(got, *two))
        two = with_own(second, half, offset, *behind(both_ways(two), *one))
    one, two = both_ways(one), both_ways(two)
    return first(0) + one[0] + one[1], second(0) + two[0] + two[1], extra


def shards(ancestor_inverse, factor_panel, pattern, diagonal_inverse):
    yl, z, x, yh, core = (lax.axis_index(name) for name in AXES)
    count, rows, cols = factor_panel.shape
    row, col = yl * 8 + z, x * 4 + yh * 2 + core
    per = rows // BLK
    keep_rows = row_mask(pattern, row, per).astype(jnp.bfloat16)
    keep_cols = row_mask(pattern, col, per).astype(jnp.float32)
    own = factor_panel.transpose(0, 2, 1) * keep_rows[:, None, :]
    near, far = send(own, swap), send(own, swap_far)
    near, far, turned, ancestor = together(near, far, send(own, skewed), ancestor_inverse)
    beside = [send(piece, across) for piece in jnp.split(ancestor, (rows // 2, rows * 5 // 6))]
    plane = jnp.stack([near, far], axis=1)
    left, right = send(plane, along_x(1)), send(plane, along_x(3))
    turned = send(turned, facing_place)
    left, right, _, beside[0] = together(left, right, turned, beside[0])
    facing = [lax.all_gather(turned, "z", axis=1), None]
    opposite = send(left[:, :1], along_x(1)), send(right[:, 1:], along_x(3))
    *opposite, beside[1] = together(*opposite, beside[1])
    own_rows = (x // 2) == yl
    mine = pair_rows(x, own_rows, plane, left, right, opposite)

    def product(panel):
        panel = panel.reshape(2, count * 4 * cols, rows)
        whole = dot_nt(panel[0], ancestor_inverse) + dot_nt(panel[1], beside)
        return whole.reshape(count, 4, cols, rows)

    theirs, beside[2] = together(send(mine, sibling), beside[2])
    beside = jnp.concatenate(beside)
    near, far = product(mine), product(theirs)
    column = jnp.where(own_rows, x % 2, 1 - x % 2)
    wide = cols // 2

    def block(first, offset):
        place = (z + offset) % 8
        at = (place // 4 ^ column) * 2 + (place // 2 % 2 ^ yh)
        start, size = (0, at, first, 0), (count, 1, wide, rows)
        picked = (lax.dynamic_slice(side, start, size) for side in (near, far))
        return jnp.where(place % 2 == core, *picked).reshape(count, wide, rows)

    chunks = [lambda offset, first=first: block(first, offset) for first in (0, wide)]
    *reduced, facing[0] = sum_over_z(*chunks, wide // 2, facing[0])
    facing[1] = send(facing[0], across)
    reduced = jnp.concatenate(reduced, axis=1)
    offdiag = -(reduced * keep_cols[:, None, :])
    high = lax.reduce_precision(reduced, 8, 7)
    parts = jnp.stack([high, reduced - high], axis=1).astype(jnp.bfloat16)
    parts = parts.reshape(count, 2 * cols, rows)
    tiles = []
    for panel in facing:
        square = dot_each(panel.reshape(count, 8 * cols, rows), parts)
        tiles.append(square[..., :cols] + square[..., cols:])
    tiles = jnp.concatenate(tiles, axis=2).reshape(count, 2, 2, 2, cols, 2 * cols)
    tiles = tiles[:, :, :, 0] + send(tiles[:, :, :, 1], sibling)
    kept, given = ordered((x // 2) == yl, tiles[..., :cols], tiles[..., cols:])
    kept, given = (jnp.concatenate([t[:, :, :, :wide], t[:, :, :, wide:]], axis=4) for t in (kept, given))
    packed = kept[:, 0] + send(kept[:, 1], flip_x(1))
    packed += send(given[:, 0], flip_x(2)) + send(given[:, 1], flip_x(3))
    packed = packed[:, 0] + send(packed[:, 1], over_y)
    diagonal = jnp.concatenate([packed[..., :cols], packed[..., cols:]], axis=1)
    diagonal += diagonal_inverse
    return offdiag.transpose(0, 2, 1), diagonal


def solution(mesh):
    fine = Mesh(mesh.devices.reshape(DIMS), AXES)
    prow, pcol = ("yl", "z"), ("x", "yh", "core")
    in_specs = (P(pcol, prow), P(None, prow, pcol), P(), P(None, pcol, prow))
    out_specs = (P(None, pcol, prow), P(None, pcol, prow))
    return jax.shard_map(shards, mesh=fine, in_specs=in_specs, out_specs=out_specs, check_vma=False)
```

```python
import jax
import jax.numpy as jnp
import numpy as np
from jax import lax
from jax.sharding import Mesh, PartitionSpec as P

BLK = 128
AXES = ("yl", "z", "x", "yh", "core")
DIMS = (2, 8, 4, 2, 2)
NT = (((1,), (1,)), ((), ()))


def pairs(move):
    grid = np.arange(256).reshape(DIMS)
    return [(int(grid[at]), int(grid[move(*at)])) for at in np.ndindex(*DIMS)]


def send(value, move):
    return lax.ppermute(value, AXES, pairs(move))


def swap(yl, z, x, yh, c):
    return (yl, z, x, yh, c) if x // 2 == yl else (1 - yl, z, 3 - x, yh, c)


def swap_far(yl, z, x, yh, c):
    return over_y(*swap(yl, z, x, yh, c))


def along_x(step):
    return lambda yl, z, x, yh, c: (yl, z, (x + step) % 4, yh, c)


def along_z(step):
    return lambda yl, z, x, yh, c: (yl, (z + step) % 8, x, yh, c)


def sibling(yl, z, x, yh, c):
    return yl, z, x, yh, 1 - c


def across(yl, z, x, yh, c):
    return 1 - yl, z, x, yh, c


def skewed(yl, z, x, yh, c):
    return yl, z ^ (x % 2 * 4 + yh * 2 + c), x, yh, c


def facing_place(yl, z, x, yh, c):
    place = z ^ (x % 2 * 4 + yh * 2 + c)
    return x // 2, z, yl * 2 + place // 4, place // 2 % 2, place % 2


def turned_place(*place):
    return facing_place(*skewed(*place))


def over_y(yl, z, x, yh, c):
    return yl, z, x, 1 - yh, c


def flip_x(bits):
    return lambda yl, z, x, yh, c: (yl, z, x ^ bits, yh, c)


def row_mask(pattern, block, per):
    picked = lax.dynamic_slice_in_dim(pattern, block * per, per, 1)
    return jnp.repeat(picked, BLK, axis=1)


def dot_nt(a, b):
    return lax.dot_general(a, b, NT, preferred_element_type=jnp.float32)


def ordered(first, near, far):
    return jnp.where(first, near, far), jnp.where(first, far, near)


def together(*values):
    return lax.optimization_barrier(values)


def dot_each(a, b):
    return jnp.einsum("knr,kmr->knm", a, b, preferred_element_type=jnp.float32)


def pair_rows(x, own_rows, plane, left, right, opposite):
    mirror, other = ordered(x % 2 == 0, left, right)
    here = ordered(own_rows, plane, mirror)
    there = ordered(own_rows, other, jnp.concatenate(opposite, axis=1))
    return jnp.stack([jnp.stack([here[h], there[h]], axis=1) for h in range(2)])


def with_own(block, half, offset, down, up):
    below, above = block(-offset), block(offset)
    if offset < 3:
        return below + down, above + up
    down = jnp.concatenate([below[:, :half] + down, below[:, half:]], axis=1)
    up = jnp.concatenate([above[:, :half], above[:, half:] + up], axis=1)
    return down, up


def sum_over_z(first, second, half):
    def both_ways(pair):
        return send(pair[0], along_z(-1)), send(pair[1], along_z(1))

    def behind(pair, *others):
        return together(*pair, *others)[:2]

    one, two = ((block(4)[:, :half], block(4)[:, half:]) for block in (first, second))
    for offset in (3, 2, 1):
        one = with_own(first, half, offset, *behind(both_ways(one), *two))
        two = with_own(second, half, offset, *behind(both_ways(two), *one))
    one, two = both_ways(one), both_ways(two)
    return first(0) + one[0] + one[1], second(0) + two[0] + two[1]


def shards(ancestor_inverse, factor_panel, pattern, diagonal_inverse):
    yl, z, x, yh, core = (lax.axis_index(name) for name in AXES)
    count, rows, cols = factor_panel.shape
    row, col = yl * 8 + z, x * 4 + yh * 2 + core
    per = rows // BLK
    keep_rows = row_mask(pattern, row, per).astype(jnp.bfloat16)
    keep_cols = row_mask(pattern, col, per).astype(jnp.float32)
    own = factor_panel.transpose(0, 2, 1) * keep_rows[:, None, :]
    near, far = send(own, swap), send(own, swap_far)
    near, far, turned, ancestor = together(near, far, send(own, turned_place), ancestor_inverse)
    beside = [send(piece, across) for piece in jnp.split(ancestor, (rows // 2, rows * 5 // 6))]
    plane = jnp.stack([near, far], axis=1)
    left, right = send(plane, along_x(1)), send(plane, along_x(3))
    left, right, beside[0] = together(left, right, beside[0])
    facing = [lax.all_gather(turned, "z", axis=1), None]
    opposite = send(left[:, :1], along_x(1)), send(right[:, 1:], along_x(3))
    *opposite, beside[1] = together(*opposite, beside[1])
    own_rows = (x // 2) == yl
    mine = pair_rows(x, own_rows, plane, left, right, opposite)

    def product(panel):
        panel = panel.reshape(2, count * 4 * cols, rows)
        whole = dot_nt(panel[0], ancestor_inverse) + dot_nt(panel[1], beside)
        return whole.reshape(count, 4, cols, rows)

    theirs, beside[2], facing[0] = together(send(mine, sibling), beside[2], facing[0])
    beside = jnp.concatenate(beside)
    near, far = product(mine), product(theirs)
    column = jnp.where(own_rows, x % 2, 1 - x % 2)
    wide = cols // 2

    def block(first, offset):
        place = (z + offset) % 8
        at = (place // 4 ^ column) * 2 + (place // 2 % 2 ^ yh)
        start, size = (0, at, first, 0), (count, 1, wide, rows)
        picked = (lax.dynamic_slice(side, start, size) for side in (near, far))
        return jnp.where(place % 2 == core, *picked).reshape(count, wide, rows)

    chunks = [lambda offset, first=first: block(first, offset) for first in (0, wide)]
    reduced = sum_over_z(*chunks, wide // 2)
    facing[1] = send(facing[0], across)
    reduced = jnp.concatenate(reduced, axis=1)
    offdiag = -(reduced * keep_cols[:, None, :])
    high = lax.reduce_precision(reduced, 8, 7)
    parts = jnp.stack([high, reduced - high], axis=1).astype(jnp.bfloat16)
    parts = parts.reshape(count, 2 * cols, rows)
    tiles = []
    for panel in facing:
        square = dot_each(panel.reshape(count, 8 * cols, rows), parts)
        tiles.append(square[..., :cols] + square[..., cols:])
    tiles = jnp.concatenate(tiles, axis=2).reshape(count, 2, 2, 2, cols, 2 * cols)
    tiles = tiles[:, :, :, 0] + send(tiles[:, :, :, 1], sibling)
    kept, given = ordered((x // 2) == yl, tiles[..., :cols], tiles[..., cols:])
    kept, given = (jnp.concatenate([t[:, :, :, :wide], t[:, :, :, wide:]], axis=4) for t in (kept, given))
    packed = kept[:, 0] + send(kept[:, 1], flip_x(1))
    packed += send(given[:, 0], flip_x(2)) + send(given[:, 1], flip_x(3))
    packed = packed[:, 0] + send(packed[:, 1], over_y)
    diagonal = jnp.concatenate([packed[..., :cols], packed[..., cols:]], axis=1)
    diagonal += diagonal_inverse
    return offdiag.transpose(0, 2, 1), diagonal


def solution(mesh):
    fine = Mesh(mesh.devices.reshape(DIMS), AXES)
    prow, pcol = ("yl", "z"), ("x", "yh", "core")
    in_specs = (P(pcol, prow), P(None, prow, pcol), P(), P(None, pcol, prow))
    out_specs = (P(None, pcol, prow), P(None, pcol, prow))
    return jax.shard_map(shards, mesh=fine, in_specs=in_specs, out_specs=out_specs, check_vma=False)
```

```python
import jax
import jax.numpy as jnp
import numpy as np
from jax import lax
from jax.sharding import Mesh, PartitionSpec as P

BLK = 128
AXES = ("yl", "z", "x", "yh", "core")
DIMS = (2, 8, 4, 2, 2)
NT = (((1,), (1,)), ((), ()))


def pairs(move):
    grid = np.arange(256).reshape(DIMS)
    return [(int(grid[at]), int(grid[move(*at)])) for at in np.ndindex(*DIMS)]


def send(value, move):
    return lax.ppermute(value, AXES, pairs(move))


def swap(yl, z, x, yh, c):
    return (yl, z, x, yh, c) if x // 2 == yl else (1 - yl, z, 3 - x, yh, c)


def swap_far(yl, z, x, yh, c):
    return over_y(*swap(yl, z, x, yh, c))


def along_x(step):
    return lambda yl, z, x, yh, c: (yl, z, (x + step) % 4, yh, c)


def along_z(step):
    return lambda yl, z, x, yh, c: (yl, (z + step) % 8, x, yh, c)


def sibling(yl, z, x, yh, c):
    return yl, z, x, yh, 1 - c


def across(yl, z, x, yh, c):
    return 1 - yl, z, x, yh, c


def skewed(yl, z, x, yh, c):
    return yl, z ^ (x % 2 * 4 + yh * 2 + c), x, yh, c


def facing_place(yl, z, x, yh, c):
    place = z ^ (x % 2 * 4 + yh * 2 + c)
    return x // 2, z, yl * 2 + place // 4, place // 2 % 2, place % 2


def turned_place(*place):
    return facing_place(*skewed(*place))


def over_y(yl, z, x, yh, c):
    return yl, z, x, 1 - yh, c


def flip_x(bits):
    return lambda yl, z, x, yh, c: (yl, z, x ^ bits, yh, c)


def row_mask(pattern, block, per):
    picked = lax.dynamic_slice_in_dim(pattern, block * per, per, 1)
    return jnp.repeat(picked, BLK, axis=1)


def dot_nt(a, b):
    return lax.dot_general(a, b, NT, preferred_element_type=jnp.float32)


def ordered(first, near, far):
    return jnp.where(first, near, far), jnp.where(first, far, near)


def together(*values):
    return lax.optimization_barrier(values)


def dot_each(a, b):
    return jnp.einsum("knr,kmr->knm", a, b, preferred_element_type=jnp.float32)


def pair_rows(x, own_rows, plane, left, right, opposite):
    mirror, other = ordered(x % 2 == 0, left, right)
    here = ordered(own_rows, plane, mirror)
    there = ordered(own_rows, other, jnp.concatenate(opposite, axis=1))
    return jnp.stack([jnp.stack([here[h], there[h]], axis=1) for h in range(2)])


def with_own(block, half, offset, down, up):
    below, above = block(-offset), block(offset)
    if offset < 3:
        return below + down, above + up
    down = jnp.concatenate([below[:, :half] + down, below[:, half:]], axis=1)
    up = jnp.concatenate([above[:, :half], above[:, half:] + up], axis=1)
    return down, up


def sum_over_z(first, second, half, beside):
    def both_ways(pair):
        return send(pair[0], along_z(-1)), send(pair[1], along_z(1))

    def behind(pair, *others):
        return together(*pair, *others)[:2]

    one, two = ((block(4)[:, :half], block(4)[:, half:]) for block in (first, second))
    for offset in (3, 2, 1):
        one = with_own(first, half, offset, *behind(both_ways(one), *two))
        two = with_own(second, half, offset, *behind(both_ways(two), *one))
    *two, beside = together(*two, beside)
    one, two = both_ways(one), both_ways(two)
    return first(0) + one[0] + one[1], second(0) + two[0] + two[1], beside


def shards(ancestor_inverse, factor_panel, pattern, diagonal_inverse):
    yl, z, x, yh, core = (lax.axis_index(name) for name in AXES)
    count, rows, cols = factor_panel.shape
    row, col = yl * 8 + z, x * 4 + yh * 2 + core
    per = rows // BLK
    keep_rows = row_mask(pattern, row, per).astype(jnp.bfloat16)
    keep_cols = row_mask(pattern, col, per).astype(jnp.float32)
    own = factor_panel.transpose(0, 2, 1) * keep_rows[:, None, :]
    near, far = send(own, swap), send(own, swap_far)
    near, far, turned, ancestor = together(near, far, send(own, turned_place), ancestor_inverse)
    beside = [send(piece, across) for piece in jnp.split(ancestor, (rows * 2 // 3,))]
    plane = jnp.stack([near, far], axis=1)
    left, right = send(plane, along_x(1)), send(plane, along_x(3))
    left, right, beside[0] = together(left, right, beside[0])
    facing = [lax.all_gather(turned, "z", axis=1), None]
    opposite = send(left[:, :1], along_x(1)), send(right[:, 1:], along_x(3))
    *opposite, beside[1] = together(*opposite, beside[1])
    own_rows = (x // 2) == yl
    mine = pair_rows(x, own_rows, plane, left, right, opposite)

    def product(panel):
        panel = panel.reshape(2, count * 4 * cols, rows)
        whole = dot_nt(panel[0], ancestor_inverse) + dot_nt(panel[1], beside)
        return whole.reshape(count, 4, cols, rows)

    theirs, facing[0] = together(send(mine, sibling), facing[0])
    beside = jnp.concatenate(beside)
    near, far = product(mine), product(theirs)
    column = jnp.where(own_rows, x % 2, 1 - x % 2)
    wide = cols // 2

    def block(first, offset):
        place = (z + offset) % 8
        at = (place // 4 ^ column) * 2 + (place // 2 % 2 ^ yh)
        start, size = (0, at, first, 0), (count, 1, wide, rows)
        picked = (lax.dynamic_slice(side, start, size) for side in (near, far))
        return jnp.where(place % 2 == core, *picked).reshape(count, wide, rows)

    chunks = [lambda offset, first=first: block(first, offset) for first in (0, wide)]
    *reduced, facing[1] = sum_over_z(*chunks, wide // 2, send(facing[0], across))
    reduced = jnp.concatenate(reduced, axis=1)
    offdiag = -(reduced * keep_cols[:, None, :])
    high = lax.reduce_precision(reduced, 8, 7)
    parts = jnp.stack([high, reduced - high], axis=1).astype(jnp.bfloat16)
    parts = parts.reshape(count, 2 * cols, rows)
    tiles = []
    for panel in facing:
        square = dot_each(panel.reshape(count, 8 * cols, rows), parts)
        tiles.append(square[..., :cols] + square[..., cols:])
    tiles = jnp.concatenate(tiles, axis=2).reshape(count, 2, 2, 2, cols, 2 * cols)
    tiles = tiles[:, :, :, 0] + send(tiles[:, :, :, 1], sibling)
    kept, given = ordered((x // 2) == yl, tiles[..., :cols], tiles[..., cols:])
    kept, given = (jnp.concatenate([t[:, :, :, :wide], t[:, :, :, wide:]], axis=4) for t in (kept, given))
    packed = kept[:, 0] + send(kept[:, 1], flip_x(1))
    packed += send(given[:, 0], flip_x(2)) + send(given[:, 1], flip_x(3))
    packed = packed[:, 0] + send(packed[:, 1], over_y)
    diagonal = jnp.concatenate([packed[..., :cols], packed[..., cols:]], axis=1)
    diagonal += diagonal_inverse
    return offdiag.transpose(0, 2, 1), diagonal


def solution(mesh):
    fine = Mesh(mesh.devices.reshape(DIMS), AXES)
    prow, pcol = ("yl", "z"), ("x", "yh", "core")
    in_specs = (P(pcol, prow), P(None, prow, pcol), P(), P(None, pcol, prow))
    out_specs = (P(None, pcol, prow), P(None, pcol, prow))
    return jax.shard_map(shards, mesh=fine, in_specs=in_specs, out_specs=out_specs, check_vma=False)
```

```python
import jax
import jax.numpy as jnp
import numpy as np
from jax import lax
from jax.sharding import Mesh, PartitionSpec as P

BLK = 128
AXES = ("yl", "z", "x", "yh", "core")
DIMS = (2, 8, 4, 2, 2)
NT = (((1,), (1,)), ((), ()))


def pairs(move):
    grid = np.arange(256).reshape(DIMS)
    return [(int(grid[at]), int(grid[move(*at)])) for at in np.ndindex(*DIMS)]


def send(value, move):
    return lax.ppermute(value, AXES, pairs(move))


def swap(yl, z, x, yh, c):
    return (yl, z, x, yh, c) if x // 2 == yl else (1 - yl, z, 3 - x, yh, c)


def swap_far(yl, z, x, yh, c):
    return over_y(*swap(yl, z, x, yh, c))


def along_x(step):
    return lambda yl, z, x, yh, c: (yl, z, (x + step) % 4, yh, c)


def along_z(step):
    return lambda yl, z, x, yh, c: (yl, (z + step) % 8, x, yh, c)


def sibling(yl, z, x, yh, c):
    return yl, z, x, yh, 1 - c


def across(yl, z, x, yh, c):
    return 1 - yl, z, x, yh, c


def skewed(yl, z, x, yh, c):
    return yl, z ^ (x % 2 * 4 + yh * 2 + c), x, yh, c


def facing_place(yl, z, x, yh, c):
    place = z ^ (x % 2 * 4 + yh * 2 + c)
    return x // 2, z, yl * 2 + place // 4, place // 2 % 2, place % 2


def turned_place(*place):
    return facing_place(*skewed(*place))


def over_y(yl, z, x, yh, c):
    return yl, z, x, 1 - yh, c


def flip_x(bits):
    return lambda yl, z, x, yh, c: (yl, z, x ^ bits, yh, c)


def row_mask(pattern, block, per):
    picked = lax.dynamic_slice_in_dim(pattern, block * per, per, 1)
    return jnp.repeat(picked, BLK, axis=1)


def dot_nt(a, b):
    return lax.dot_general(a, b, NT, preferred_element_type=jnp.float32)


def ordered(first, near, far):
    return jnp.where(first, near, far), jnp.where(first, far, near)


def together(*values):
    return lax.optimization_barrier(values)


def dot_each(a, b):
    return jnp.einsum("knr,kmr->knm", a, b, preferred_element_type=jnp.float32)


def pair_rows(x, own_rows, plane, left, right, opposite):
    mirror, other = ordered(x % 2 == 0, left, right)
    here = ordered(own_rows, plane, mirror)
    there = ordered(own_rows, other, jnp.concatenate(opposite, axis=1))
    return jnp.stack([jnp.stack([here[h], there[h]], axis=1) for h in range(2)])


def with_own(block, half, offset, down, up):
    below, above = block(-offset), block(offset)
    if offset < 3:
        return below + down, above + up
    down = jnp.concatenate([below[:, :half] + down, below[:, half:]], axis=1)
    up = jnp.concatenate([above[:, :half], above[:, half:] + up], axis=1)
    return down, up


def sum_over_z(first, second, half, beside):
    def both_ways(pair):
        return send(pair[0], along_z(-1)), send(pair[1], along_z(1))

    def behind(pair, *others):
        return together(*pair, *others)[:2]

    one, two = ((block(4)[:, :half], block(4)[:, half:]) for block in (first, second))
    for offset in (3, 2, 1):
        one = with_own(first, half, offset, *behind(both_ways(one), *two))
        two = with_own(second, half, offset, *behind(both_ways(two), *one))
    one, two = both_ways(one), both_ways(two)
    *two, beside = together(*two, beside)
    return first(0) + one[0] + one[1], second(0) + two[0] + two[1], beside


def shards(ancestor_inverse, factor_panel, pattern, diagonal_inverse):
    yl, z, x, yh, core = (lax.axis_index(name) for name in AXES)
    count, rows, cols = factor_panel.shape
    row, col = yl * 8 + z, x * 4 + yh * 2 + core
    per = rows // BLK
    keep_rows = row_mask(pattern, row, per).astype(jnp.bfloat16)
    keep_cols = row_mask(pattern, col, per).astype(jnp.float32)
    own = factor_panel.transpose(0, 2, 1) * keep_rows[:, None, :]
    near, far = send(own, swap), send(own, swap_far)
    near, far, turned, ancestor = together(near, far, send(own, turned_place), ancestor_inverse)
    beside = [send(piece, across) for piece in jnp.split(ancestor, (rows * 2 // 3,))]
    plane = jnp.stack([near, far], axis=1)
    left, right = send(plane, along_x(1)), send(plane, along_x(3))
    left, right, beside[0] = together(left, right, beside[0])
    facing = [lax.all_gather(turned, "z", axis=1), None]
    opposite = send(left[:, :1], along_x(1)), send(right[:, 1:], along_x(3))
    *opposite, beside[1] = together(*opposite, beside[1])
    own_rows = (x // 2) == yl
    mine = pair_rows(x, own_rows, plane, left, right, opposite)

    def product(panel):
        panel = panel.reshape(2, count * 4 * cols, rows)
        whole = dot_nt(panel[0], ancestor_inverse) + dot_nt(panel[1], beside)
        return whole.reshape(count, 4, cols, rows)

    theirs, facing[0] = together(send(mine, sibling), facing[0])
    beside = jnp.concatenate(beside)
    near, far = product(mine), product(theirs)
    column = jnp.where(own_rows, x % 2, 1 - x % 2)
    wide = cols // 2

    def block(first, offset):
        place = (z + offset) % 8
        at = (place // 4 ^ column) * 2 + (place // 2 % 2 ^ yh)
        start, size = (0, at, first, 0), (count, 1, wide, rows)
        picked = (lax.dynamic_slice(side, start, size) for side in (near, far))
        return jnp.where(place % 2 == core, *picked).reshape(count, wide, rows)

    chunks = [lambda offset, first=first: block(first, offset) for first in (0, wide)]
    *reduced, facing[1] = sum_over_z(*chunks, wide // 2, send(facing[0], across))
    reduced = jnp.concatenate(reduced, axis=1)
    offdiag = -(reduced * keep_cols[:, None, :])
    high = lax.reduce_precision(reduced, 8, 7)
    parts = jnp.stack([high, reduced - high], axis=1).astype(jnp.bfloat16)
    parts = parts.reshape(count, 2 * cols, rows)
    tiles = []
    for panel in facing:
        square = dot_each(panel.reshape(count, 8 * cols, rows), parts)
        tiles.append(square[..., :cols] + square[..., cols:])
    tiles = jnp.concatenate(tiles, axis=2).reshape(count, 2, 2, 2, cols, 2 * cols)
    tiles = tiles[:, :, :, 0] + send(tiles[:, :, :, 1], sibling)
    kept, given = ordered((x // 2) == yl, tiles[..., :cols], tiles[..., cols:])
    kept, given = (jnp.concatenate([t[:, :, :, :wide], t[:, :, :, wide:]], axis=4) for t in (kept, given))
    packed = kept[:, 0] + send(kept[:, 1], flip_x(1))
    packed += send(given[:, 0], flip_x(2)) + send(given[:, 1], flip_x(3))
    packed = packed[:, 0] + send(packed[:, 1], over_y)
    diagonal = jnp.concatenate([packed[..., :cols], packed[..., cols:]], axis=1)
    diagonal += diagonal_inverse
    return offdiag.transpose(0, 2, 1), diagonal


def solution(mesh):
    fine = Mesh(mesh.devices.reshape(DIMS), AXES)
    prow, pcol = ("yl", "z"), ("x", "yh", "core")
    in_specs = (P(pcol, prow), P(None, prow, pcol), P(), P(None, pcol, prow))
    out_specs = (P(None, pcol, prow), P(None, pcol, prow))
    return jax.shard_map(shards, mesh=fine, in_specs=in_specs, out_specs=out_specs, check_vma=False)
```

```python
import jax
import jax.numpy as jnp
import numpy as np
from jax import lax
from jax.sharding import Mesh, PartitionSpec as P

BLK = 128
AXES = ("yl", "z", "x", "yh", "core")
DIMS = (2, 8, 4, 2, 2)
NT = (((1,), (1,)), ((), ()))


def pairs(move):
    grid = np.arange(256).reshape(DIMS)
    return [(int(grid[at]), int(grid[move(*at)])) for at in np.ndindex(*DIMS)]


def send(value, move):
    return lax.ppermute(value, AXES, pairs(move))


def swap(yl, z, x, yh, c):
    return (yl, z, x, yh, c) if x // 2 == yl else (1 - yl, z, 3 - x, yh, c)


def swap_far(yl, z, x, yh, c):
    return over_y(*swap(yl, z, x, yh, c))


def along_x(step):
    return lambda yl, z, x, yh, c: (yl, z, (x + step) % 4, yh, c)


def along_z(step):
    return lambda yl, z, x, yh, c: (yl, (z + step) % 8, x, yh, c)


def sibling(yl, z, x, yh, c):
    return yl, z, x, yh, 1 - c


def across(yl, z, x, yh, c):
    return 1 - yl, z, x, yh, c


def skewed(yl, z, x, yh, c):
    return yl, z ^ (x % 2 * 4 + yh * 2 + c), x, yh, c


def facing_place(yl, z, x, yh, c):
    place = z ^ (x % 2 * 4 + yh * 2 + c)
    return x // 2, z, yl * 2 + place // 4, place // 2 % 2, place % 2


def turned_place(*place):
    return facing_place(*skewed(*place))


def over_y(yl, z, x, yh, c):
    return yl, z, x, 1 - yh, c


def flip_x(bits):
    return lambda yl, z, x, yh, c: (yl, z, x ^ bits, yh, c)


def row_mask(pattern, block, per):
    picked = lax.dynamic_slice_in_dim(pattern, block * per, per, 1)
    return jnp.repeat(picked, BLK, axis=1)


def dot_nt(a, b):
    return lax.dot_general(a, b, NT, preferred_element_type=jnp.float32)


def ordered(first, near, far):
    return jnp.where(first, near, far), jnp.where(first, far, near)


def together(*values):
    return lax.optimization_barrier(values)


def dot_each(a, b):
    return jnp.einsum("knr,kmr->knm", a, b, preferred_element_type=jnp.float32)


def pair_rows(x, own_rows, plane, left, right, opposite):
    mirror, other = ordered(x % 2 == 0, left, right)
    here = ordered(own_rows, plane, mirror)
    there = ordered(own_rows, other, jnp.concatenate(opposite, axis=1))
    return jnp.stack([jnp.stack([here[h], there[h]], axis=1) for h in range(2)])


def with_own(block, half, offset, down, up):
    below, above = block(-offset), block(offset)
    if offset < 3:
        return below + down, above + up
    down = jnp.concatenate([below[:, :half] + down, below[:, half:]], axis=1)
    up = jnp.concatenate([above[:, :half], above[:, half:] + up], axis=1)
    return down, up


def sum_over_z(first, second, half, beside):
    def both_ways(pair):
        return send(pair[0], along_z(-1)), send(pair[1], along_z(1))

    def behind(pair, *others):
        return together(*pair, *others)[:2]

    one, two = ((block(4)[:, :half], block(4)[:, half:]) for block in (first, second))
    for offset in (3, 2, 1):
        one = with_own(first, half, offset, *behind(both_ways(one), *two))
        two = with_own(second, half, offset, *behind(both_ways(two), *one))
    one, two = both_ways(one), both_ways(two)
    *two, beside = together(*two, beside)
    return first(0) + one[0] + one[1], second(0) + two[0] + two[1], beside


def shards(ancestor_inverse, factor_panel, pattern, diagonal_inverse):
    yl, z, x, yh, core = (lax.axis_index(name) for name in AXES)
    count, rows, cols = factor_panel.shape
    row, col = yl * 8 + z, x * 4 + yh * 2 + core
    per = rows // BLK
    keep_rows = row_mask(pattern, row, per).astype(jnp.bfloat16)
    keep_cols = row_mask(pattern, col, per).astype(jnp.float32)
    own = factor_panel.transpose(0, 2, 1) * keep_rows[:, None, :]
    near, far = send(own, swap), send(own, swap_far)
    pieces = jnp.split(ancestor_inverse, (rows // 2,))
    near, far, turned, *pieces = together(near, far, send(own, turned_place), *pieces)
    plane = jnp.stack([near, far], axis=1)
    left, right = send(plane, along_x(1)), send(plane, along_x(3))
    beside = [send(piece, across) for piece in pieces]
    left, right, beside[0] = together(left, right, beside[0])
    facing = [lax.all_gather(turned, "z", axis=1), None]
    opposite = send(left[:, :1], along_x(1)), send(right[:, 1:], along_x(3))
    *opposite, beside[1] = together(*opposite, beside[1])
    own_rows = (x // 2) == yl
    mine = pair_rows(x, own_rows, plane, left, right, opposite)

    def product(panel):
        panel = panel.reshape(2, count * 4 * cols, rows)
        whole = dot_nt(panel[0], ancestor_inverse) + dot_nt(panel[1], beside)
        return whole.reshape(count, 4, cols, rows)

    theirs, facing[0] = together(send(mine, sibling), facing[0])
    beside = jnp.concatenate(beside)
    near, far = product(mine), product(theirs)
    column = jnp.where(own_rows, x % 2, 1 - x % 2)
    wide = cols // 2

    def block(first, offset):
        place = (z + offset) % 8
        at = (place // 4 ^ column) * 2 + (place // 2 % 2 ^ yh)
        start, size = (0, at, first, 0), (count, 1, wide, rows)
        picked = (lax.dynamic_slice(side, start, size) for side in (near, far))
        return jnp.where(place % 2 == core, *picked).reshape(count, wide, rows)

    chunks = [lambda offset, first=first: block(first, offset) for first in (0, wide)]
    *reduced, facing[1] = sum_over_z(*chunks, wide // 2, send(facing[0], across))
    reduced = jnp.concatenate(reduced, axis=1)
    offdiag = -(reduced * keep_cols[:, None, :])
    high = lax.reduce_precision(reduced, 8, 7)
    parts = jnp.stack([high, reduced - high], axis=1).astype(jnp.bfloat16)
    parts = parts.reshape(count, 2 * cols, rows)
    tiles = []
    for panel in facing:
        square = dot_each(panel.reshape(count, 8 * cols, rows), parts)
        tiles.append(square[..., :cols] + square[..., cols:])
    tiles = jnp.concatenate(tiles, axis=2).reshape(count, 2, 2, 2, cols, 2 * cols)
    tiles = tiles[:, :, :, 0] + send(tiles[:, :, :, 1], sibling)
    kept, given = ordered((x // 2) == yl, tiles[..., :cols], tiles[..., cols:])
    kept, given = (jnp.concatenate([t[:, :, :, :wide], t[:, :, :, wide:]], axis=4) for t in (kept, given))
    packed = kept[:, 0] + send(kept[:, 1], flip_x(1))
    packed += send(given[:, 0], flip_x(2)) + send(given[:, 1], flip_x(3))
    packed = packed[:, 0] + send(packed[:, 1], over_y)
    diagonal = jnp.concatenate([packed[..., :cols], packed[..., cols:]], axis=1)
    diagonal += diagonal_inverse
    return offdiag.transpose(0, 2, 1), diagonal


def solution(mesh):
    fine = Mesh(mesh.devices.reshape(DIMS), AXES)
    prow, pcol = ("yl", "z"), ("x", "yh", "core")
    in_specs = (P(pcol, prow), P(None, prow, pcol), P(), P(None, pcol, prow))
    out_specs = (P(None, pcol, prow), P(None, pcol, prow))
    return jax.shard_map(shards, mesh=fine, in_specs=in_specs, out_specs=out_specs, check_vma=False)
```

```python
import jax
import jax.numpy as jnp
import numpy as np
from jax import lax
from jax.sharding import Mesh, PartitionSpec as P

BLK = 128
AXES = ("yl", "z", "x", "yh", "core")
DIMS = (2, 8, 4, 2, 2)
NT = (((1,), (1,)), ((), ()))


def pairs(move):
    grid = np.arange(256).reshape(DIMS)
    return [(int(grid[at]), int(grid[move(*at)])) for at in np.ndindex(*DIMS)]


def send(value, move):
    return lax.ppermute(value, AXES, pairs(move))


def swap(yl, z, x, yh, c):
    return (yl, z, x, yh, c) if x // 2 == yl else (1 - yl, z, 3 - x, yh, c)


def swap_far(yl, z, x, yh, c):
    return over_y(*swap(yl, z, x, yh, c))


def along_x(step):
    return lambda yl, z, x, yh, c: (yl, z, (x + step) % 4, yh, c)


def along_z(step):
    return lambda yl, z, x, yh, c: (yl, (z + step) % 8, x, yh, c)


def sibling(yl, z, x, yh, c):
    return yl, z, x, yh, 1 - c


def across(yl, z, x, yh, c):
    return 1 - yl, z, x, yh, c


def skewed(yl, z, x, yh, c):
    return yl, z ^ (x % 2 * 4 + yh * 2 + c), x, yh, c


def facing_place(yl, z, x, yh, c):
    place = z ^ (x % 2 * 4 + yh * 2 + c)
    return x // 2, z, yl * 2 + place // 4, place // 2 % 2, place % 2


def turned_place(*place):
    return facing_place(*skewed(*place))


def over_y(yl, z, x, yh, c):
    return yl, z, x, 1 - yh, c


def flip_plane(bits, bit):
    return lambda yl, z, x, yh, c: (yl, z, x ^ bits, yh ^ bit, c)


def row_mask(pattern, block, per):
    picked = lax.dynamic_slice_in_dim(pattern, block * per, per, 1)
    return jnp.repeat(picked, BLK, axis=1)


def dot_nt(a, b):
    return lax.dot_general(a, b, NT, preferred_element_type=jnp.float32)


def ordered(first, near, far):
    return jnp.where(first, near, far), jnp.where(first, far, near)


def together(*values):
    return lax.optimization_barrier(values)


def dot_each(a, b):
    return jnp.einsum("knr,kmr->knm", a, b, preferred_element_type=jnp.float32)


def pair_rows(x, own_rows, plane, left, right, opposite):
    mirror, other = ordered(x % 2 == 0, left, right)
    here = ordered(own_rows, plane, mirror)
    there = ordered(own_rows, other, jnp.concatenate(opposite, axis=1))
    return jnp.stack([jnp.stack([here[h], there[h]], axis=1) for h in range(2)])


def with_own(block, half, offset, down, up):
    below, above = block(-offset), block(offset)
    if offset < 3:
        return below + down, above + up
    down = jnp.concatenate([below[:, :half] + down, below[:, half:]], axis=1)
    up = jnp.concatenate([above[:, :half], above[:, half:] + up], axis=1)
    return down, up


def sum_over_z(first, second, half, beside):
    def both_ways(pair):
        return send(pair[0], along_z(-1)), send(pair[1], along_z(1))

    def behind(pair, *others):
        return together(*pair, *others)[:2]

    one, two = ((block(4)[:, :half], block(4)[:, half:]) for block in (first, second))
    for offset in (3, 2, 1):
        one = with_own(first, half, offset, *behind(both_ways(one), *two))
        two = with_own(second, half, offset, *behind(both_ways(two), *one))
    one, two = both_ways(one), both_ways(two)
    *two, beside = together(*two, beside)
    return first(0) + one[0] + one[1], second(0) + two[0] + two[1], beside


def shards(ancestor_inverse, factor_panel, pattern, diagonal_inverse):
    yl, z, x, yh, core = (lax.axis_index(name) for name in AXES)
    count, rows, cols = factor_panel.shape
    row, col = yl * 8 + z, x * 4 + yh * 2 + core
    per = rows // BLK
    keep_rows = row_mask(pattern, row, per).astype(jnp.bfloat16)
    keep_cols = row_mask(pattern, col, per).astype(jnp.float32)
    own = factor_panel.transpose(0, 2, 1) * keep_rows[:, None, :]
    near, far = send(own, swap), send(own, swap_far)
    pieces = jnp.split(ancestor_inverse, (rows // 2,))
    near, far, turned, *pieces = together(near, far, send(own, turned_place), *pieces)
    plane = jnp.stack([near, far], axis=1)
    left, right = send(plane, along_x(1)), send(plane, along_x(3))
    beside = [send(piece, across) for piece in pieces]
    left, right, beside[0] = together(left, right, beside[0])
    facing = [lax.all_gather(turned, "z", axis=1), None]
    opposite = send(left[:, :1], along_x(1)), send(right[:, 1:], along_x(3))
    *opposite, beside[1] = together(*opposite, beside[1])
    own_rows = (x // 2) == yl
    mine = pair_rows(x, own_rows, plane, left, right, opposite)

    def product(panel):
        panel = panel.reshape(2, count * 4 * cols, rows)
        whole = dot_nt(panel[0], ancestor_inverse) + dot_nt(panel[1], beside)
        return whole.reshape(count, 4, cols, rows)

    theirs, facing[0] = together(send(mine, sibling), facing[0])
    beside = jnp.concatenate(beside)
    near, far = product(mine), product(theirs)
    column = jnp.where(own_rows, x % 2, 1 - x % 2)
    wide = cols // 2

    def block(first, offset):
        place = (z + offset) % 8
        at = (place // 4 ^ column) * 2 + (place // 2 % 2 ^ yh)
        start, size = (0, at, first, 0), (count, 1, wide, rows)
        picked = (lax.dynamic_slice(side, start, size) for side in (near, far))
        return jnp.where(place % 2 == core, *picked).reshape(count, wide, rows)

    chunks = [lambda offset, first=first: block(first, offset) for first in (0, wide)]
    *reduced, facing[1] = sum_over_z(*chunks, wide // 2, send(facing[0], across))
    reduced = jnp.concatenate(reduced, axis=1)
    offdiag = -(reduced * keep_cols[:, None, :])
    high = lax.reduce_precision(reduced, 8, 7)
    parts = jnp.stack([high, reduced - high], axis=1).astype(jnp.bfloat16)
    parts = parts.reshape(count, 2 * cols, rows)
    tiles = []
    for panel in facing:
        square = dot_each(panel.reshape(count, 8 * cols, rows), parts)
        tiles.append(square[..., :cols] + square[..., cols:])
    tiles = jnp.concatenate(tiles, axis=2).reshape(count, 2, 2, 2, cols, 2 * cols)
    tiles = tiles[:, :, :, 0] + send(tiles[:, :, :, 1], sibling)
    kept, given = ordered((x // 2) == yl, tiles[..., :cols], tiles[..., cols:])
    kept, given = (jnp.concatenate([t[:, :, :, :wide], t[:, :, :, wide:]], axis=4) for t in (kept, given))
    packed = kept[:, 0, 0]
    for bits in range(1, 8):
        side = given if bits & 4 else kept
        packed += send(side[:, bits >> 1 & 1, bits & 1], flip_plane(bits >> 1, bits & 1))
    diagonal = jnp.concatenate([packed[..., :cols], packed[..., cols:]], axis=1)
    diagonal += diagonal_inverse
    return offdiag.transpose(0, 2, 1), diagonal


def solution(mesh):
    fine = Mesh(mesh.devices.reshape(DIMS), AXES)
    prow, pcol = ("yl", "z"), ("x", "yh", "core")
    in_specs = (P(pcol, prow), P(None, prow, pcol), P(), P(None, pcol, prow))
    out_specs = (P(None, pcol, prow), P(None, pcol, prow))
    return jax.shard_map(shards, mesh=fine, in_specs=in_specs, out_specs=out_specs, check_vma=False)
```

```python
import jax
import jax.numpy as jnp
import numpy as np
from jax import lax
from jax.sharding import Mesh, PartitionSpec as P

BLK = 128
AXES = ("yl", "z", "x", "yh", "core")
DIMS = (2, 8, 4, 2, 2)
NT = (((1,), (1,)), ((), ()))


def pairs(move):
    grid = np.arange(256).reshape(DIMS)
    return [(int(grid[at]), int(grid[move(*at)])) for at in np.ndindex(*DIMS)]


def send(value, move):
    return lax.ppermute(value, AXES, pairs(move))


def swap(yl, z, x, yh, c):
    return (yl, z, x, yh, c) if x // 2 == yl else (1 - yl, z, 3 - x, yh, c)


def swap_far(yl, z, x, yh, c):
    return over_y(*swap(yl, z, x, yh, c))


def along_x(step):
    return lambda yl, z, x, yh, c: (yl, z, (x + step) % 4, yh, c)


def along_z(step):
    return lambda yl, z, x, yh, c: (yl, (z + step) % 8, x, yh, c)


def sibling(yl, z, x, yh, c):
    return yl, z, x, yh, 1 - c


def across(yl, z, x, yh, c):
    return 1 - yl, z, x, yh, c


def skewed(yl, z, x, yh, c):
    return yl, z ^ (x % 2 * 4 + yh * 2 + c), x, yh, c


def facing_place(yl, z, x, yh, c):
    place = z ^ (x % 2 * 4 + yh * 2 + c)
    return x // 2, z, yl * 2 + place // 4, place // 2 % 2, place % 2


def turned_place(*place):
    return facing_place(*skewed(*place))


def over_y(yl, z, x, yh, c):
    return yl, z, x, 1 - yh, c


def flip_x(bits):
    return lambda yl, z, x, yh, c: (yl, z, x ^ bits, yh, c)


def row_mask(pattern, block, per):
    picked = lax.dynamic_slice_in_dim(pattern, block * per, per, 1)
    return jnp.repeat(picked, BLK, axis=1)


def dot_nt(a, b):
    return lax.dot_general(a, b, NT, preferred_element_type=jnp.float32)


def ordered(first, near, far):
    return jnp.where(first, near, far), jnp.where(first, far, near)


def together(*values):
    return lax.optimization_barrier(values)


def dot_each(a, b):
    return jnp.einsum("knr,kmr->knm", a, b, preferred_element_type=jnp.float32)


def pair_rows(x, own_rows, plane, left, right, opposite):
    mirror, other = ordered(x % 2 == 0, left, right)
    here = ordered(own_rows, plane, mirror)
    there = ordered(own_rows, other, jnp.concatenate(opposite, axis=1))
    return jnp.stack([jnp.stack([here[h], there[h]], axis=1) for h in range(2)])


def with_own(block, half, offset, down, up):
    below, above = block(-offset), block(offset)
    if offset < 3:
        return below + down, above + up
    down = jnp.concatenate([below[:, :half] + down, below[:, half:]], axis=1)
    up = jnp.concatenate([above[:, :half], above[:, half:] + up], axis=1)
    return down, up


def sum_over_z(first, second, half, beside):
    def both_ways(pair):
        return send(pair[0], along_z(-1)), send(pair[1], along_z(1))

    def behind(pair, *others):
        return together(*pair, *others)[:2]

    one, two = ((block(4)[:, :half], block(4)[:, half:]) for block in (first, second))
    for offset in (3, 2, 1):
        one = with_own(first, half, offset, *behind(both_ways(one), *two))
        two = with_own(second, half, offset, *behind(both_ways(two), *one))
    one, two = both_ways(one), both_ways(two)
    *two, beside = together(*two, beside)
    return first(0) + one[0] + one[1], second(0) + two[0] + two[1], beside


def shards(ancestor_inverse, factor_panel, pattern, diagonal_inverse):
    yl, z, x, yh, core = (lax.axis_index(name) for name in AXES)
    count, rows, cols = factor_panel.shape
    row, col = yl * 8 + z, x * 4 + yh * 2 + core
    per = rows // BLK
    keep_rows = row_mask(pattern, row, per).astype(jnp.bfloat16)
    keep_cols = row_mask(pattern, col, per).astype(jnp.float32)
    own = factor_panel.transpose(0, 2, 1) * keep_rows[:, None, :]
    near, far = send(own, swap), send(own, swap_far)
    pieces = jnp.split(ancestor_inverse, (rows * 7 // 12,))
    near, far, turned, *pieces = together(near, far, send(own, turned_place), *pieces)
    plane = jnp.stack([near, far], axis=1)
    left, right = send(plane, along_x(1)), send(plane, along_x(3))
    beside = [send(pieces[0], across), None]
    left, right, beside[0], last = together(left, right, beside[0], pieces[1])
    beside[1] = send(last, across)
    facing = [lax.all_gather(turned, "z", axis=1), None]
    opposite = send(left[:, :1], along_x(1)), send(right[:, 1:], along_x(3))
    *opposite, beside[1] = together(*opposite, beside[1])
    own_rows = (x // 2) == yl
    mine = pair_rows(x, own_rows, plane, left, right, opposite)

    def product(panel):
        panel = [side.reshape(count * 4 * cols, rows) for side in panel]
        whole = dot_nt(panel[0], ancestor_inverse) + dot_nt(panel[1], beside)
        return whole.reshape(count, 4, cols, rows)

    theirs = list(send(mine, sibling))
    theirs[1], facing[0] = together(theirs[1], facing[0])
    beside = jnp.concatenate(beside)
    near, far = product(mine), product(theirs)
    column = jnp.where(own_rows, x % 2, 1 - x % 2)
    wide = cols // 2

    def block(first, offset):
        place = (z + offset) % 8
        at = (place // 4 ^ column) * 2 + (place // 2 % 2 ^ yh)
        start, size = (0, at, first, 0), (count, 1, wide, rows)
        picked = (lax.dynamic_slice(side, start, size) for side in (near, far))
        return jnp.where(place % 2 == core, *picked).reshape(count, wide, rows)

    chunks = [lambda offset, first=first: block(first, offset) for first in (0, wide)]
    *reduced, facing[1] = sum_over_z(*chunks, wide // 2, send(facing[0], across))
    reduced = jnp.concatenate(reduced, axis=1)
    offdiag = -(reduced * keep_cols[:, None, :])
    high = lax.reduce_precision(reduced, 8, 7)
    parts = jnp.stack([high, reduced - high], axis=1).astype(jnp.bfloat16)
    parts = parts.reshape(count, 2 * cols, rows)
    tiles = []
    for panel in facing:
        square = dot_each(panel.reshape(count, 8 * cols, rows), parts)
        tiles.append(square[..., :cols] + square[..., cols:])
    tiles = jnp.concatenate(tiles, axis=2).reshape(count, 2, 2, 2, cols, 2 * cols)
    tiles = tiles[:, :, :, 0] + send(tiles[:, :, :, 1], sibling)
    kept, given = ordered((x // 2) == yl, tiles[..., :cols], tiles[..., cols:])
    kept, given = (jnp.concatenate([t[:, :, :, :wide], t[:, :, :, wide:]], axis=4) for t in (kept, given))
    packed = kept[:, 0] + send(kept[:, 1], flip_x(1))
    packed += send(given[:, 0], flip_x(2)) + send(given[:, 1], flip_x(3))
    packed = packed[:, 0] + send(packed[:, 1], over_y)
    diagonal = jnp.concatenate([packed[..., :cols], packed[..., cols:]], axis=1)
    diagonal += diagonal_inverse
    return offdiag.transpose(0, 2, 1), diagonal


def solution(mesh):
    fine = Mesh(mesh.devices.reshape(DIMS), AXES)
    prow, pcol = ("yl", "z"), ("x", "yh", "core")
    in_specs = (P(pcol, prow), P(None, prow, pcol), P(), P(None, pcol, prow))
    out_specs = (P(None, pcol, prow), P(None, pcol, prow))
    return jax.shard_map(shards, mesh=fine, in_specs=in_specs, out_specs=out_specs, check_vma=False)
```
